32 devices in a mesh: hid: 16 (over z, y, x), seq: 2 (over core).
Axes of the slice: x: 2, y: 2, z: 4, core: 2. Of those that a mesh axis runs over, the one named last changes fastest.
Arguments:
- pre_act: bfloat16 [192, 4096], P(('hid', 'seq')), may hold values from -6 to 6
- butterfly: bfloat16 [16, 5, 256, 256], P('hid'), may hold values from -0.15625 to 0.15625
- low_u: bfloat16 [4096, 256], P('hid'), may hold values from -0.75 to 0.75
- low_v: bfloat16 [256, 4096], P(None, 'hid'), may hold values from -0.1875 to 0.1875
- grad_out: bfloat16 [192, 4096], P(('hid', 'seq')), may hold values from -6 to 6
Outputs:
- output: bfloat16 [192, 4096], P(('hid', 'seq'))
- grad_pre: bfloat16 [192, 4096], P(('hid', 'seq'))
- grad_butterfly: float32 [16, 5, 256, 256], P('hid', None, 'seq')
- grad_low_u: float32 [4096, 256], P('hid', 'seq')
- grad_low_v: float32 [256, 4096], P('seq', 'hid')
The draws below stay inside these ranges and needn't reach their ends.
All inputs are finite; a program needn't handle non-finite values.
Results may differ from the reference program's by a relative error of at most 0.0075.
Values may be sent and summed in bfloat16 or wider, within the bound.
No kernel may reach another device: no remote copies, remote signals or barrier semaphores. Data moves between devices by JAX's collectives and lax.ppermute only.
A program may use at most 64 MiB of HBM per device.

```python
import math
import jax
import jax.numpy as jnp
import numpy as np

B = 256
LEVELS = 4
R = 256
FF = 4096
BLOCKS = 16
TOKENS = 192


def block_levels(rng, shape, shards, least, top_value):
    loudness, own = 1.0, jax.random.fold_in(rng, 6)
    for axis_at, shards_of in shards:
        heights = jnp.exp(jax.random.uniform(jax.random.fold_in(own, axis_at), (shards_of,), jnp.float32, least / len(shards), top_value / len(shards)))
        loudness = loudness * jnp.repeat(heights, shape[axis_at] // shards_of).reshape([-1 if axis == axis_at else 1 for axis in range(len(shape))])
    return loudness


def noise(stream_key, extent, deviation, most, shards=(), dtype=jnp.bfloat16):
    array = deviation * jax.random.normal(stream_key, extent, jnp.float32)
    if shards:
        array = array * block_levels(stream_key, extent, shards, -0.22, 0.18)
    return jnp.clip(array, -most, most).astype(dtype)


def setup_inputs(seed: int = 0) -> dict:
    arg_keys = jax.random.split(jax.random.key(seed), 6)
    return {
        "pre_act": noise(arg_keys[0], (TOKENS, FF), 1.0, 6.0, ((0, 32),)),
        "butterfly": noise(arg_keys[1], (BLOCKS, LEVELS + 1, B, B), ((LEVELS + 1) * B) ** -0.5, 0.15625, ((0, 16),)),
        "low_u": noise(arg_keys[2], (FF, R), (FF // 64) ** -0.5, 0.75, ((0, 16),)),
        "low_v": noise(arg_keys[3], (R, FF), (FF // 4) ** -0.5, 0.1875, ((1, 16),)),
        "grad_out": noise(arg_keys[4], (TOKENS, FF), 1.0, 6.0, ((0, 32),)),
    }


def gelu_tanh(value):
    return jax.nn.gelu(value, approximate=True)

def reference(pre_act, butterfly, low_u, low_v, grad_out):
    pre_f = pre_act.astype(jnp.float32)
    act = gelu_tanh(pre_f).astype(jnp.bfloat16)
    latent = jnp.dot(act, low_u, preferred_element_type=jnp.float32).astype(jnp.bfloat16)
    act_blocks = act.reshape(TOKENS, BLOCKS, B)
    grad_blocks = grad_out.reshape(TOKENS, BLOCKS, B)
    grad_float = grad_blocks.astype(jnp.float32)
    order = np.arange(BLOCKS)
    total = jnp.dot(latent, low_v, preferred_element_type=jnp.float32).reshape(TOKENS, BLOCKS, B)
    backward = jnp.zeros((TOKENS, BLOCKS, B), jnp.float32)
    weight_grads = []
    for level in range(LEVELS + 1):
        source = order if level == 0 else order ^ 1 << level - 1
        moved = act_blocks[:, source, :].astype(jnp.float32)
        weights = butterfly[:, level].astype(jnp.float32)
        total = total + jnp.einsum('tjb,jbc->tjc', moved, weights)
        grad_moved = grad_float[:, source, :]
        weights_moved = butterfly[source, level].astype(jnp.float32)
        backward = backward + jnp.einsum('tic,ibc->tib', grad_moved, weights_moved)
        weight_grads.append(jnp.einsum('tjb,tjc->jbc', moved, grad_float))
    output = total.reshape(TOKENS, FF).astype(jnp.bfloat16)
    dlatent = jnp.dot(grad_out, low_v.T, preferred_element_type=jnp.float32).astype(jnp.bfloat16)
    backward = backward.reshape(TOKENS, FF) + jnp.dot(dlatent, low_u.T, preferred_element_type=jnp.float32)
    grad_act = backward.astype(jnp.bfloat16)
    unused, pullback = jax.vjp(gelu_tanh, pre_f)
    grad_pre = pullback(grad_act.astype(jnp.float32))[0].astype(jnp.bfloat16)
    factor = 1.0 / math.sqrt(TOKENS)
    grad_butterfly = jnp.stack(weight_grads, axis=1) * factor
    grad_low_u = jnp.dot(act.T, dlatent, preferred_element_type=jnp.float32) * factor
    grad_low_v = jnp.dot(latent.T, grad_out, preferred_element_type=jnp.float32) * factor
    return (output, grad_pre, grad_butterfly, grad_low_u, grad_low_v)
```

```python
import math

import jax
import jax.numpy as jnp
from jax import lax
from jax.sharding import PartitionSpec as P


def exchange(x, mask):
    return lax.ppermute(x, "hid", [(i, i ^ mask) for i in range(lax.axis_size("hid"))])


def mate(x):
    return lax.ppermute(x, "seq", [(0, 1), (1, 0)])


def gelu_tanh(value):
    return jax.nn.gelu(value, approximate=True)


def dot(left, right):
    return jnp.dot(left, right, preferred_element_type=jnp.float32)


def dot_t(left, right):
    return lax.dot_general(
        left, right, (((1,), (1,)), ((), ())), preferred_element_type=jnp.float32
    )


def inner_rows(left, right):
    return lax.dot_general(
        left, right, (((0,), (0,)), ((), ())), preferred_element_type=jnp.float32
    )


def sum_over_hid(part):
    bits = (lax.axis_size("hid") - 1).bit_length()
    total = part
    for low in range(0, bits, 2):
        sent = total.astype(jnp.bfloat16)
        masks = [1 << low]
        if low + 1 < bits:
            masks += [2 << low, 3 << low]
        total = total + sum(exchange(sent, mask).astype(jnp.float32) for mask in masks)
    return total.astype(jnp.bfloat16)


def half(x, which):
    width = x.shape[1] // 2
    return jnp.where(which == 0, x[:, :width], x[:, width:])


def on_device(pre_act, butterfly, low_u, low_v, grad_out):
    tokens = pre_act.shape[0]
    hid = lax.axis_size("hid")
    core = lax.axis_index("seq")
    side = butterfly.shape[-1]
    levels = butterfly.shape[1] - 1
    rank = low_u.shape[1]
    factor = 1.0 / math.sqrt(tokens * hid * lax.axis_size("seq"))

    both = jnp.concatenate(
        [pre_act.reshape(tokens, hid, side), grad_out.reshape(tokens, hid, side)], axis=2
    ).reshape(tokens, hid * 2 * side)
    rows = lax.all_to_all(both, "hid", split_axis=1, concat_axis=0, tiled=True)
    pre_f = rows[:, :side].astype(jnp.float32)
    grad = rows[:, side:]
    act_f, pullback = jax.vjp(gelu_tanh, pre_f)
    act = act_f.astype(jnp.bfloat16)

    latents = sum_over_hid(jnp.concatenate([dot(act, low_u), dot_t(grad, low_v)], axis=1))
    latent, dlatent = latents[:, :rank], latents[:, rank:]

    acts = [act]
    total = dot(act, butterfly[0, 0])
    back = dot_t(grad, butterfly[0, 0])
    for level in range(1, levels + 1):
        term = dot_t(grad, butterfly[0, level]).astype(jnp.bfloat16)
        far = exchange(jnp.concatenate([act, term], axis=1), 1 << level - 1)
        acts.append(far[:, :side])
        total = total + dot(far[:, :side], butterfly[0, level])
        back = back + far[:, side:].astype(jnp.float32)

    output_rows = (total + dot(latent, low_v)).astype(jnp.bfloat16)
    grad_act = (back + dot_t(dlatent, low_u)).astype(jnp.bfloat16)
    grad_pre_rows = pullback(grad_act.astype(jnp.float32))[0].astype(jnp.bfloat16)
    results = jnp.concatenate([output_rows, grad_pre_rows], axis=1)
    results = lax.all_to_all(results, "hid", split_axis=0, concat_axis=1, tiled=True)
    results = results.reshape(tokens, hid, 2 * side)
    output = results[:, :, :side].reshape(tokens, hid * side)
    grad_pre = results[:, :, side:].reshape(tokens, hid * side)

    other = 1 - core
    sent = jnp.concatenate(
        [grad, act] + [half(x, other) for x in acts[1:]], axis=1
    )
    got = mate(sent)
    own = jnp.concatenate([half(x, core) for x in acts], axis=1)
    far = jnp.concatenate(
        [half(got[:, side : 2 * side], core), got[:, 2 * side :]], axis=1
    )
    grad_butterfly = (inner_rows(own, grad) + inner_rows(far, got[:, :side])) * factor
    grad_butterfly = grad_butterfly.reshape(1, levels + 1, side // 2, side)
    far_latents = mate(jnp.concatenate([half(latent, other), half(dlatent, other)], axis=1))
    far_latent, far_dlatent = far_latents[:, : rank // 2], far_latents[:, rank // 2 :]
    grad_low_u = (
        inner_rows(act, half(dlatent, core)) + inner_rows(got[:, side : 2 * side], far_dlatent)
    ) * factor
    grad_low_v = (
        inner_rows(half(latent, core), grad) + inner_rows(far_latent, got[:, :side])
    ) * factor
    return (output, grad_pre, grad_butterfly, grad_low_u, grad_low_v)


def solution(mesh):
    in_specs = (
        P(("hid", "seq"), None),
        P("hid", None, None, None),
        P("hid", None),
        P(None, "hid"),
        P(("hid", "seq"), None),
    )
    out_specs = (
        P(("hid", "seq"), None),
        P(("hid", "seq"), None),
        P("hid", None, "seq", None),
        P("hid", "seq"),
        P("seq", "hid"),
    )
    return jax.shard_map(
        on_device, mesh=mesh, in_specs=in_specs, out_specs=out_specs, check_vma=False
    )
```

```python
import math

import jax
import jax.numpy as jnp
from jax import lax
from jax.sharding import PartitionSpec as P


def exchange(x, mask):
    return lax.ppermute(x, "hid", [(i, i ^ mask) for i in range(lax.axis_size("hid"))])


def mate(x):
    return lax.ppermute(x, "seq", [(0, 1), (1, 0)])


def gelu_tanh(value):
    return jax.nn.gelu(value, approximate=True)


def dot(left, right):
    return jnp.dot(left, right, preferred_element_type=jnp.float32)


def dot_t(left, right):
    return lax.dot_general(
        left, right, (((1,), (1,)), ((), ())), preferred_element_type=jnp.float32
    )


def inner_rows(left, right):
    return lax.dot_general(
        left, right, (((0,), (0,)), ((), ())), preferred_element_type=jnp.float32
    )


def split_hid():
    hid = lax.axis_size("hid")
    low = 1 << ((hid - 1).bit_length() // 2)
    return hid // low, low


def swap_slow(x):
    high, low = split_hid()
    groups = [[i * low + j for i in range(high)] for j in range(low)]
    return lax.all_to_all(x, "hid", 0, 0, axis_index_groups=groups, tiled=True)


def swap_fast(x):
    high, low = split_hid()
    groups = [[i * low + j for j in range(low)] for i in range(high)]
    return lax.all_to_all(x, "hid", 0, 0, axis_index_groups=groups, tiled=True)


def sum_over_hid(part):
    high, low = split_hid()
    tokens, width = part.shape
    pieces = part.astype(jnp.bfloat16).reshape(low, tokens // low, width)
    piece = jnp.sum(swap_fast(pieces).astype(jnp.float32), axis=0).astype(jnp.bfloat16)
    pieces = swap_slow(jnp.broadcast_to(piece[None], (high,) + piece.shape))
    piece = jnp.sum(pieces.astype(jnp.float32), axis=0).astype(jnp.bfloat16)
    pieces = swap_fast(jnp.broadcast_to(piece[None], (low,) + piece.shape))
    return pieces.reshape(tokens, width)


def half(x, which):
    width = x.shape[1] // 2
    return jnp.where(which == 0, x[:, :width], x[:, width:])


def on_device(pre_act, butterfly, low_u, low_v, grad_out):
    tokens = pre_act.shape[0]
    hid = lax.axis_size("hid")
    core = lax.axis_index("seq")
    side = butterfly.shape[-1]
    levels = butterfly.shape[1] - 1
    rank = low_u.shape[1]
    factor = 1.0 / math.sqrt(tokens * hid * lax.axis_size("seq"))

    high, low = split_hid()
    both = jnp.concatenate(
        [pre_act.reshape(tokens, high, low, side), grad_out.reshape(tokens, high, low, side)],
        axis=3,
    )
    rows = swap_fast(both.transpose(2, 1, 0, 3))
    rows = swap_slow(rows.transpose(1, 0, 2, 3)).reshape(hid * tokens, 2 * side)
    pre_f = rows[:, :side].astype(jnp.float32)
    grad = rows[:, side:]
    act_f, pullback = jax.vjp(gelu_tanh, pre_f)
    act = act_f.astype(jnp.bfloat16)

    latents = sum_over_hid(jnp.concatenate([dot(act, low_u), dot_t(grad, low_v)], axis=1))
    latent, dlatent = latents[:, :rank], latents[:, rank:]

    acts = [act]
    total = dot(act, butterfly[0, 0])
    back = dot_t(grad, butterfly[0, 0])
    for level in range(1, levels + 1):
        term = dot_t(grad, butterfly[0, level]).astype(jnp.bfloat16)
        far = exchange(jnp.concatenate([act, term], axis=1), 1 << level - 1)
        acts.append(far[:, :side])
        total = total + dot(far[:, :side], butterfly[0, level])
        back = back + far[:, side:].astype(jnp.float32)

    output_rows = (total + dot(latent, low_v)).astype(jnp.bfloat16)
    grad_act = (back + dot_t(dlatent, low_u)).astype(jnp.bfloat16)
    grad_pre_rows = pullback(grad_act.astype(jnp.float32))[0].astype(jnp.bfloat16)
    results = jnp.concatenate([output_rows, grad_pre_rows], axis=1)
    results = swap_slow(results.reshape(high, low, tokens, 2 * side))
    results = swap_fast(results.transpose(1, 0, 2, 3))
    results = results.transpose(2, 1, 0, 3).reshape(tokens, hid, 2 * side)
    output = results[:, :, :side].reshape(tokens, hid * side)
    grad_pre = results[:, :, side:].reshape(tokens, hid * side)

    other = 1 - core
    sent = jnp.concatenate(
        [grad, act] + [half(x, other) for x in acts[1:]], axis=1
    )
    got = mate(sent)
    own = jnp.concatenate([half(x, core) for x in acts], axis=1)
    far = jnp.concatenate(
        [half(got[:, side : 2 * side], core), got[:, 2 * side :]], axis=1
    )
    grad_butterfly = (inner_rows(own, grad) + inner_rows(far, got[:, :side])) * factor
    grad_butterfly = grad_butterfly.reshape(1, levels + 1, side // 2, side)
    far_latents = mate(jnp.concatenate([half(latent, other), half(dlatent, other)], axis=1))
    far_latent, far_dlatent = far_latents[:, : rank // 2], far_latents[:, rank // 2 :]
    grad_low_u = (
        inner_rows(act, half(dlatent, core)) + inner_rows(got[:, side : 2 * side], far_dlatent)
    ) * factor
    grad_low_v = (
        inner_rows(half(latent, core), grad) + inner_rows(far_latent, got[:, :side])
    ) * factor
    return (output, grad_pre, grad_butterfly, grad_low_u, grad_low_v)


def solution(mesh):
    in_specs = (
        P(("hid", "seq"), None),
        P("hid", None, None, None),
        P("hid", None),
        P(None, "hid"),
        P(("hid", "seq"), None),
    )
    out_specs = (
        P(("hid", "seq"), None),
        P(("hid", "seq"), None),
        P("hid", None, "seq", None),
        P("hid", "seq"),
        P("seq", "hid"),
    )
    return jax.shard_map(
        on_device, mesh=mesh, in_specs=in_specs, out_specs=out_specs, check_vma=False
    )
```

```python
import math

import jax
import jax.numpy as jnp
from jax import lax
from jax.sharding import PartitionSpec as P


def exchange(x, mask):
    return lax.ppermute(x, "hid", [(i, i ^ mask) for i in range(lax.axis_size("hid"))])


def mate(x):
    return lax.ppermute(x, "seq", [(0, 1), (1, 0)])


def gelu_tanh(value):
    return jax.nn.gelu(value, approximate=True)


def dot(left, right):
    return jnp.dot(left, right, preferred_element_type=jnp.float32)


def dot_t(left, right):
    return lax.dot_general(
        left, right, (((1,), (1,)), ((), ())), preferred_element_type=jnp.float32
    )


def inner_rows(left, right):
    return lax.dot_general(
        left, right, (((0,), (0,)), ((), ())), preferred_element_type=jnp.float32
    )


def sum_over_hid(part):
    hid = lax.axis_size("hid")
    low = 1 << ((hid - 1).bit_length() // 2)
    rows = part.shape[0] // low
    place = lax.axis_index("hid") % low
    sent = part.astype(jnp.bfloat16)

    def take(x, at):
        return lax.dynamic_slice_in_dim(x, at * rows, rows, 0)

    piece = take(part, place)
    got = [exchange(take(sent, place ^ mask), mask) for mask in range(1, low)]
    got = lax.optimization_barrier(got)
    piece = piece + sum(x.astype(jnp.float32) for x in got)
    sent = piece.astype(jnp.bfloat16)
    got = [exchange(sent, mask) for mask in range(low, hid, low)]
    got = lax.optimization_barrier(got)
    piece = (piece + sum(x.astype(jnp.float32) for x in got)).astype(jnp.bfloat16)
    got = [exchange(piece, mask) for mask in range(1, low)]
    total = jnp.zeros(part.shape, jnp.bfloat16)
    for mask, x in enumerate(lax.optimization_barrier([piece] + got)):
        total = lax.dynamic_update_slice_in_dim(total, x, (place ^ mask) * rows, 0)
    return total


def half(x, which):
    width = x.shape[1] // 2
    return jnp.where(which == 0, x[:, :width], x[:, width:])


def on_device(pre_act, butterfly, low_u, low_v, grad_out):
    tokens = pre_act.shape[0]
    hid = lax.axis_size("hid")
    core = lax.axis_index("seq")
    side = butterfly.shape[-1]
    levels = butterfly.shape[1] - 1
    rank = low_u.shape[1]
    factor = 1.0 / math.sqrt(tokens * hid * lax.axis_size("seq"))

    both = jnp.concatenate(
        [pre_act.reshape(tokens, hid, side), grad_out.reshape(tokens, hid, side)], axis=2
    ).reshape(tokens, hid * 2 * side)
    rows = lax.all_to_all(both, "hid", split_axis=1, concat_axis=0, tiled=True)
    pre_f = rows[:, :side].astype(jnp.float32)
    grad = rows[:, side:]
    act_f, pullback = jax.vjp(gelu_tanh, pre_f)
    act = act_f.astype(jnp.bfloat16)

    latents = sum_over_hid(jnp.concatenate([dot(act, low_u), dot_t(grad, low_v)], axis=1))
    latent, dlatent = latents[:, :rank], latents[:, rank:]

    acts = [act]
    total = dot(act, butterfly[0, 0])
    back = dot_t(grad, butterfly[0, 0])
    for level in range(1, levels + 1):
        term = dot_t(grad, butterfly[0, level]).astype(jnp.bfloat16)
        far = exchange(jnp.concatenate([act, term], axis=1), 1 << level - 1)
        acts.append(far[:, :side])
        total = total + dot(far[:, :side], butterfly[0, level])
        back = back + far[:, side:].astype(jnp.float32)

    output_rows = (total + dot(latent, low_v)).astype(jnp.bfloat16)
    grad_act = (back + dot_t(dlatent, low_u)).astype(jnp.bfloat16)
    grad_pre_rows = pullback(grad_act.astype(jnp.float32))[0].astype(jnp.bfloat16)
    results = jnp.concatenate([output_rows, grad_pre_rows], axis=1)
    other = 1 - core
    sent = jnp.concatenate(
        [grad, act] + [half(x, other) for x in acts[1:]], axis=1
    )
    sent_latents = jnp.concatenate([half(latent, other), half(dlatent, other)], axis=1)
    results, sent, sent_latents = lax.optimization_barrier((results, sent, sent_latents))
    results = lax.all_to_all(results, "hid", split_axis=0, concat_axis=1, tiled=True)
    results = results.reshape(tokens, hid, 2 * side)
    output = results[:, :, :side].reshape(tokens, hid * side)
    grad_pre = results[:, :, side:].reshape(tokens, hid * side)

    got = mate(sent)
    own = jnp.concatenate([half(x, core) for x in acts], axis=1)
    far = jnp.concatenate(
        [half(got[:, side : 2 * side], core), got[:, 2 * side :]], axis=1
    )
    grad_butterfly = (inner_rows(own, grad) + inner_rows(far, got[:, :side])) * factor
    grad_butterfly = grad_butterfly.reshape(1, levels + 1, side // 2, side)
    far_latents = mate(sent_latents)
    far_latent, far_dlatent = far_latents[:, : rank // 2], far_latents[:, rank // 2 :]
    grad_low_u = (
        inner_rows(act, half(dlatent, core)) + inner_rows(got[:, side : 2 * side], far_dlatent)
    ) * factor
    grad_low_v = (
        inner_rows(half(latent, core), grad) + inner_rows(far_latent, got[:, :side])
    ) * factor
    return (output, grad_pre, grad_butterfly, grad_low_u, grad_low_v)


def solution(mesh):
    in_specs = (
        P(("hid", "seq"), None),
        P("hid", None, None, None),
        P("hid", None),
        P(None, "hid"),
        P(("hid", "seq"), None),
    )
    out_specs = (
        P(("hid", "seq"), None),
        P(("hid", "seq"), None),
        P("hid", None, "seq", None),
        P("hid", "seq"),
        P("seq", "hid"),
    )
    return jax.shard_map(
        on_device, mesh=mesh, in_specs=in_specs, out_specs=out_specs, check_vma=False
    )
```

```python
import math

import jax
import jax.numpy as jnp
from jax import lax
from jax.sharding import PartitionSpec as P


def exchange(x, mask):
    return lax.ppermute(x, "hid", [(i, i ^ mask) for i in range(lax.axis_size("hid"))])


def mate(x):
    return lax.ppermute(x, "seq", [(0, 1), (1, 0)])


def gelu_tanh(value):
    return jax.nn.gelu(value, approximate=True)


def dot(left, right):
    return jnp.dot(left, right, preferred_element_type=jnp.float32)


def dot_t(left, right):
    return lax.dot_general(
        left, right, (((1,), (1,)), ((), ())), preferred_element_type=jnp.float32
    )


def inner_rows(left, right):
    return lax.dot_general(
        left, right, (((0,), (0,)), ((), ())), preferred_element_type=jnp.float32
    )


def sum_over_hid(part, blocks):
    bits = (lax.axis_size("hid") - 1).bit_length()
    width = part.shape[1]
    total, far = part, {}
    for low in range(0, bits, 2):
        sent = total.astype(jnp.bfloat16)
        got = {}
        for mask in range(1 << low, min(4 << low, 1 << bits), 1 << low):
            if low == 0 and mask in blocks:
                got[mask] = exchange(jnp.concatenate([sent, blocks[mask]], axis=1), mask)
            else:
                got[mask] = exchange(sent, mask)
        if low == 0:
            apart = {mask: exchange(blocks[mask], mask) for mask in blocks if mask not in got}
            got = lax.optimization_barrier(got)
            far = {mask: got[mask][:, width:] for mask in blocks if mask in got}
        if low + 2 >= bits:
            got, apart = lax.optimization_barrier((got, apart))
        total = total + sum(x[:, :width].astype(jnp.float32) for x in got.values())
    far.update(apart)
    return total.astype(jnp.bfloat16), [far[mask] for mask in blocks]


def half(x, which):
    width = x.shape[1] // 2
    return jnp.where(which == 0, x[:, :width], x[:, width:])


def on_device(pre_act, butterfly, low_u, low_v, grad_out):
    tokens = pre_act.shape[0]
    hid = lax.axis_size("hid")
    core = lax.axis_index("seq")
    side = butterfly.shape[-1]
    levels = butterfly.shape[1] - 1
    rank = low_u.shape[1]
    factor = 1.0 / math.sqrt(tokens * hid * lax.axis_size("seq"))

    both = jnp.concatenate(
        [pre_act.reshape(tokens, hid, side), grad_out.reshape(tokens, hid, side)], axis=2
    ).reshape(tokens, hid * 2 * side)
    rows = lax.all_to_all(both, "hid", split_axis=1, concat_axis=0, tiled=True)
    pre_f = rows[:, :side].astype(jnp.float32)
    grad = rows[:, side:]
    act_f, pullback = jax.vjp(gelu_tanh, pre_f)
    act = act_f.astype(jnp.bfloat16)

    part = jnp.concatenate([dot(act, low_u), dot_t(grad, low_v)], axis=1)
    blocks = {}
    for level in range(1, levels + 1):
        term = dot_t(grad, butterfly[0, level]).astype(jnp.bfloat16)
        blocks[1 << level - 1] = jnp.concatenate([act, term], axis=1)
    latents, fars = sum_over_hid(part, blocks)
    latent, dlatent = latents[:, :rank], latents[:, rank:]

    acts = [act] + [far[:, :side] for far in fars]
    total = dot(jnp.concatenate(acts, axis=1), butterfly[0].reshape(-1, side))
    back = dot_t(grad, butterfly[0, 0])
    for far in fars:
        back = back + far[:, side:].astype(jnp.float32)

    output_rows = (total + dot(latent, low_v)).astype(jnp.bfloat16)
    grad_act = (back + dot_t(dlatent, low_u)).astype(jnp.bfloat16)
    grad_pre_rows = pullback(grad_act.astype(jnp.float32))[0].astype(jnp.bfloat16)
    results = jnp.concatenate([output_rows, grad_pre_rows], axis=1)
    results = lax.all_to_all(results, "hid", split_axis=0, concat_axis=1, tiled=True)
    results = results.reshape(tokens, hid, 2 * side)
    output = results[:, :, :side].reshape(tokens, hid * side)
    grad_pre = results[:, :, side:].reshape(tokens, hid * side)

    other = 1 - core
    sent = jnp.concatenate(
        [grad, act] + [half(x, other) for x in acts[1:]], axis=1
    )
    got = mate(sent)
    own = jnp.concatenate([half(x, core) for x in acts], axis=1)
    far = jnp.concatenate(
        [half(got[:, side : 2 * side], core), got[:, 2 * side :]], axis=1
    )
    grad_butterfly = (inner_rows(own, grad) + inner_rows(far, got[:, :side])) * factor
    grad_butterfly = grad_butterfly.reshape(1, levels + 1, side // 2, side)
    far_latents = mate(jnp.concatenate([half(latent, other), half(dlatent, other)], axis=1))
    far_latent, far_dlatent = far_latents[:, : rank // 2], far_latents[:, rank // 2 :]
    grad_low_u = (
        inner_rows(act, half(dlatent, core)) + inner_rows(got[:, side : 2 * side], far_dlatent)
    ) * factor
    grad_low_v = (
        inner_rows(half(latent, core), grad) + inner_rows(far_latent, got[:, :side])
    ) * factor
    return (output, grad_pre, grad_butterfly, grad_low_u, grad_low_v)


def solution(mesh):
    in_specs = (
        P(("hid", "seq"), None),
        P("hid", None, None, None),
        P("hid", None),
        P(None, "hid"),
        P(("hid", "seq"), None),
    )
    out_specs = (
        P(("hid", "seq"), None),
        P(("hid", "seq"), None),
        P("hid", None, "seq", None),
        P("hid", "seq"),
        P("seq", "hid"),
    )
    return jax.shard_map(
        on_device, mesh=mesh, in_specs=in_specs, out_specs=out_specs, check_vma=False
    )
```

```python
import math

import jax
import jax.numpy as jnp
from jax import lax
from jax.sharding import PartitionSpec as P


def exchange(x, mask):
    return lax.ppermute(x, "hid", [(i, i ^ mask) for i in range(lax.axis_size("hid"))])


def mate(x):
    return lax.ppermute(x, "seq", [(0, 1), (1, 0)])


def gelu_tanh(value):
    return jax.nn.gelu(value, approximate=True)


def dot(left, right):
    return jnp.dot(left, right, preferred_element_type=jnp.float32)


def dot_t(left, right):
    return lax.dot_general(
        left, right, (((1,), (1,)), ((), ())), preferred_element_type=jnp.float32
    )


def inner_rows(left, right):
    return lax.dot_general(
        left, right, (((0,), (0,)), ((), ())), preferred_element_type=jnp.float32
    )


def sum_over_hid(part):
    return lax.psum(part.astype(jnp.bfloat16), "hid")


def half(x, which):
    width = x.shape[1] // 2
    return jnp.where(which == 0, x[:, :width], x[:, width:])


def on_device(pre_act, butterfly, low_u, low_v, grad_out):
    tokens = pre_act.shape[0]
    hid = lax.axis_size("hid")
    core = lax.axis_index("seq")
    side = butterfly.shape[-1]
    levels = butterfly.shape[1] - 1
    rank = low_u.shape[1]
    factor = 1.0 / math.sqrt(tokens * hid * lax.axis_size("seq"))

    both = jnp.concatenate(
        [pre_act.reshape(tokens, hid, side), grad_out.reshape(tokens, hid, side)], axis=2
    ).reshape(tokens, hid * 2 * side)
    rows = lax.all_to_all(both, "hid", split_axis=1, concat_axis=0, tiled=True)
    pre_f = rows[:, :side].astype(jnp.float32)
    grad = rows[:, side:]
    act_f, pullback = jax.vjp(gelu_tanh, pre_f)
    act = act_f.astype(jnp.bfloat16)

    latents = sum_over_hid(jnp.concatenate([dot(act, low_u), dot_t(grad, low_v)], axis=1))
    latent, dlatent = latents[:, :rank], latents[:, rank:]

    acts = [act]
    total = dot(act, butterfly[0, 0])
    back = dot_t(grad, butterfly[0, 0])
    for level in range(1, levels + 1):
        term = dot_t(grad, butterfly[0, level]).astype(jnp.bfloat16)
        far = exchange(jnp.concatenate([act, term], axis=1), 1 << level - 1)
        acts.append(far[:, :side])
        total = total + dot(far[:, :side], butterfly[0, level])
        back = back + far[:, side:].astype(jnp.float32)

    output_rows = (total + dot(latent, low_v)).astype(jnp.bfloat16)
    grad_act = (back + dot_t(dlatent, low_u)).astype(jnp.bfloat16)
    grad_pre_rows = pullback(grad_act.astype(jnp.float32))[0].astype(jnp.bfloat16)
    results = jnp.concatenate([output_rows, grad_pre_rows], axis=1)
    results = lax.all_to_all(results, "hid", split_axis=0, concat_axis=1, tiled=True)
    results = results.reshape(tokens, hid, 2 * side)
    output = results[:, :, :side].reshape(tokens, hid * side)
    grad_pre = results[:, :, side:].reshape(tokens, hid * side)

    other = 1 - core
    sent = jnp.concatenate(
        [grad, act] + [half(x, other) for x in acts[1:]], axis=1
    )
    got = mate(sent)
    own = jnp.concatenate([half(x, core) for x in acts], axis=1)
    far = jnp.concatenate(
        [half(got[:, side : 2 * side], core), got[:, 2 * side :]], axis=1
    )
    grad_butterfly = (inner_rows(own, grad) + inner_rows(far, got[:, :side])) * factor
    grad_butterfly = grad_butterfly.reshape(1, levels + 1, side // 2, side)
    far_latents = mate(jnp.concatenate([half(latent, other), half(dlatent, other)], axis=1))
    far_latent, far_dlatent = far_latents[:, : rank // 2], far_latents[:, rank // 2 :]
    grad_low_u = (
        inner_rows(act, half(dlatent, core)) + inner_rows(got[:, side : 2 * side], far_dlatent)
    ) * factor
    grad_low_v = (
        inner_rows(half(latent, core), grad) + inner_rows(far_latent, got[:, :side])
    ) * factor
    return (output, grad_pre, grad_butterfly, grad_low_u, grad_low_v)


def solution(mesh):
    in_specs = (
        P(("hid", "seq"), None),
        P("hid", None, None, None),
        P("hid", None),
        P(None, "hid"),
        P(("hid", "seq"), None),
    )
    out_specs = (
        P(("hid", "seq"), None),
        P(("hid", "seq"), None),
        P("hid", None, "seq", None),
        P("hid", "seq"),
        P("seq", "hid"),
    )
    return jax.shard_map(
        on_device, mesh=mesh, in_specs=in_specs, out_specs=out_specs, check_vma=False
    )
```

```python
import math

import jax
import jax.numpy as jnp
from jax import lax
from jax.sharding import PartitionSpec as P


def exchange(x, mask):
    return lax.ppermute(x, "hid", [(i, i ^ mask) for i in range(lax.axis_size("hid"))])


def mate(x):
    return lax.ppermute(x, "seq", [(0, 1), (1, 0)])


def gelu_tanh(value):
    return jax.nn.gelu(value, approximate=True)


def dot(left, right):
    return jnp.dot(left, right, preferred_element_type=jnp.float32)


def dot_t(left, right):
    return lax.dot_general(
        left, right, (((1,), (1,)), ((), ())), preferred_element_type=jnp.float32
    )


def inner_rows(left, right):
    return lax.dot_general(
        left, right, (((0,), (0,)), ((), ())), preferred_element_type=jnp.float32
    )


def sum_over_hid(part, blocks):
    bits = (lax.axis_size("hid") - 1).bit_length()
    total, far, late = part, {}, {}
    for low in range(0, bits, 2):
        sent = total.astype(jnp.bfloat16)
        if low == 2:
            late = {mask: blocks[mask] for mask in blocks if mask not in far}
            sent, late = lax.optimization_barrier((sent, late))
        masks = [mask << low for mask in (1, 2, 3) if mask << low < 1 << bits]
        got = {mask: exchange(sent, mask) for mask in masks}
        if low == 0:
            far = {mask: exchange(blocks[mask], mask) for mask in blocks if mask not in masks}
        elif low == 2:
            late = {mask: exchange(late[mask], mask) for mask in late}
        if low + 2 < bits:
            got = lax.optimization_barrier(got)
        else:
            got, late = lax.optimization_barrier((got, late))
        total = total + sum(x.astype(jnp.float32) for x in got.values())
    return total.astype(jnp.bfloat16), far, late


def halves(x, first):
    width = x.shape[1] // 2
    low, high = x[:, :width], x[:, width:]
    return jnp.where(first, low, high), jnp.where(first, high, low)


def on_device(pre_act, butterfly, low_u, low_v, grad_out):
    tokens = pre_act.shape[0]
    hid = lax.axis_size("hid")
    first = lax.axis_index("seq") == 0
    side = butterfly.shape[-1]
    levels = butterfly.shape[1] - 1
    rank = low_u.shape[1]
    factor = 1.0 / math.sqrt(tokens * hid * lax.axis_size("seq"))

    pre_act, grad_out, first = lax.optimization_barrier((pre_act, grad_out, first))
    both = jnp.concatenate(
        [pre_act.reshape(tokens, hid, side), grad_out.reshape(tokens, hid, side)], axis=2
    ).reshape(tokens, hid * 2 * side)
    rows = lax.all_to_all(both, "hid", split_axis=1, concat_axis=0, tiled=True)
    pre_f = rows[:, :side].astype(jnp.float32)
    grad = rows[:, side:]
    act_f, pullback = jax.vjp(gelu_tanh, pre_f)
    act = act_f.astype(jnp.bfloat16)

    part = jnp.concatenate([dot(act, low_u), dot_t(grad, low_v)], axis=1)
    part, grad = lax.optimization_barrier((part, grad))
    blocks = {}
    for level in range(1, levels + 1):
        term = dot_t(grad, butterfly[0, level]).astype(jnp.bfloat16)
        blocks[1 << level - 1] = jnp.concatenate([act, term], axis=1)
    latents, early, late = sum_over_hid(part, blocks)
    fars = [(early | late)[mask] for mask in blocks]
    latent, dlatent = latents[:, :rank], latents[:, rank:]

    acts = [act] + [far[:, :side] for far in fars]
    total = dot(act, butterfly[0, 0])
    back = dot_t(grad, butterfly[0, 0])
    for level in range(1, levels + 1):
        total = total + dot(acts[level], butterfly[0, level])
        back = back + fars[level - 1][:, side:].astype(jnp.float32)

    output_rows = (total + dot(latent, low_v)).astype(jnp.bfloat16)
    grad_act = (back + dot_t(dlatent, low_u)).astype(jnp.bfloat16)
    grad_pre_rows = pullback(grad_act.astype(jnp.float32))[0].astype(jnp.bfloat16)
    results = jnp.concatenate([output_rows, grad_pre_rows], axis=1)
    results = lax.all_to_all(results, "hid", split_axis=0, concat_axis=1, tiled=True)

    def theirs(received):
        return [halves(x[:, :side], first)[1] for x in received.values()]

    def ours(received):
        return [halves(x[:, :side], first)[0] for x in received.values()]

    half = side // 2
    got = mate(jnp.concatenate([grad, act] + theirs(early), axis=1))
    far_grad, far_act = got[:, :side], got[:, side : 2 * side]
    latent, sent_latent = halves(latent, first)
    dlatent, sent_dlatent = halves(dlatent, first)
    last = mate(jnp.concatenate([sent_latent, sent_dlatent] + theirs(late), axis=1))
    far_latent, far_dlatent = last[:, : rank // 2], last[:, rank // 2 : rank]
    far = dict(zip(early, jnp.split(got[:, 2 * side :], len(early), axis=1)))
    far.update(zip(late, jnp.split(last[:, rank:], len(late), axis=1)))
    own = jnp.concatenate(ours({0: act}) + ours({mask: (early | late)[mask] for mask in blocks}), axis=1)
    far = jnp.concatenate(ours({0: far_act}) + [far[mask] for mask in blocks], axis=1)
    grad_butterfly = (inner_rows(own, grad) + inner_rows(far, far_grad)) * factor
    grad_butterfly = grad_butterfly.reshape(1, levels + 1, half, side)
    grad_low_u = (inner_rows(act, dlatent) + inner_rows(far_act, far_dlatent)) * factor
    grad_low_v = (inner_rows(latent, grad) + inner_rows(far_latent, far_grad)) * factor

    results = results.reshape(tokens, hid, 2 * side)
    output = results[:, :, :side].reshape(tokens, hid * side)
    grad_pre = results[:, :, side:].reshape(tokens, hid * side)
    return (output, grad_pre, grad_butterfly, grad_low_u, grad_low_v)


def solution(mesh):
    in_specs = (
        P(("hid", "seq"), None),
        P("hid", None, None, None),
        P("hid", None),
        P(None, "hid"),
        P(("hid", "seq"), None),
    )
    out_specs = (
        P(("hid", "seq"), None),
        P(("hid", "seq"), None),
        P("hid", None, "seq", None),
        P("hid", "seq"),
        P("seq", "hid"),
    )
    return jax.shard_map(
        on_device, mesh=mesh, in_specs=in_specs, out_specs=out_specs, check_vma=False
    )
```

```python
import math

import jax
import jax.numpy as jnp
from jax import lax
from jax.sharding import PartitionSpec as P


def exchange(x, mask):
    return lax.ppermute(x, "hid", [(i, i ^ mask) for i in range(lax.axis_size("hid"))])


def mate(x):
    return lax.ppermute(x, "seq", [(0, 1), (1, 0)])


def gelu_tanh(value):
    return jax.nn.gelu(value, approximate=True)


def dot(left, right):
    return jnp.dot(left, right, preferred_element_type=jnp.float32)


def dot_t(left, right):
    return lax.dot_general(
        left, right, (((1,), (1,)), ((), ())), preferred_element_type=jnp.float32
    )


def inner_rows(left, right):
    return lax.dot_general(
        left, right, (((0,), (0,)), ((), ())), preferred_element_type=jnp.float32
    )


def sum_over_hid(part):
    bits = (lax.axis_size("hid") - 1).bit_length()
    total = part
    for low in range(0, bits, 2):
        sent = total.astype(jnp.bfloat16)
        masks = [1 << low]
        if low + 1 < bits:
            masks += [2 << low, 3 << low]
        total = total + sum(exchange(sent, mask).astype(jnp.float32) for mask in masks)
    return total.astype(jnp.bfloat16)


def halves(x, first):
    width = x.shape[1] // 2
    low, high = x[:, :width], x[:, width:]
    return jnp.where(first, low, high), jnp.where(first, high, low)


def on_device(pre_act, butterfly, low_u, low_v, grad_out):
    tokens = pre_act.shape[0]
    hid = lax.axis_size("hid")
    first = lax.axis_index("seq") == 0
    side = butterfly.shape[-1]
    levels = butterfly.shape[1] - 1
    rank = low_u.shape[1]
    factor = 1.0 / math.sqrt(tokens * hid * lax.axis_size("seq"))

    pre_act, grad_out, first = lax.optimization_barrier((pre_act, grad_out, first))
    both = jnp.concatenate(
        [pre_act.reshape(tokens, hid, side), grad_out.reshape(tokens, hid, side)], axis=2
    ).reshape(tokens, hid * 2 * side)
    rows = lax.all_to_all(both, "hid", split_axis=1, concat_axis=0, tiled=True)
    pre_f = rows[:, :side].astype(jnp.float32)
    grad = rows[:, side:]
    act_f, pullback = jax.vjp(gelu_tanh, pre_f)
    act = act_f.astype(jnp.bfloat16)

    latents = sum_over_hid(jnp.concatenate([dot(act, low_u), dot_t(grad, low_v)], axis=1))
    latent, dlatent = latents[:, :rank], latents[:, rank:]

    acts = [act]
    total = dot(act, butterfly[0, 0])
    back = dot_t(grad, butterfly[0, 0])
    for level in range(1, levels + 1):
        term = dot_t(grad, butterfly[0, level]).astype(jnp.bfloat16)
        far = exchange(jnp.concatenate([act, term], axis=1), 1 << level - 1)
        acts.append(far[:, :side])
        total = total + dot(far[:, :side], butterfly[0, level])
        back = back + far[:, side:].astype(jnp.float32)

    output_rows = (total + dot(latent, low_v)).astype(jnp.bfloat16)
    grad_act = (back + dot_t(dlatent, low_u)).astype(jnp.bfloat16)
    grad_pre_rows = pullback(grad_act.astype(jnp.float32))[0].astype(jnp.bfloat16)
    results = jnp.concatenate([output_rows, grad_pre_rows], axis=1)
    results = lax.all_to_all(results, "hid", split_axis=0, concat_axis=1, tiled=True)
    results = results.reshape(tokens, hid, 2 * side)
    output = results[:, :, :side].reshape(tokens, hid * side)
    grad_pre = results[:, :, side:].reshape(tokens, hid * side)

    split = [halves(x, first) for x in acts[1:]]
    got = mate(jnp.concatenate([grad, act] + [theirs for ours, theirs in split[::-1]], axis=1))
    far_grad, far_act = got[:, :side], got[:, side : 2 * side]
    far_halves = jnp.split(got[:, 2 * side :], levels, axis=1)[::-1]
    latent, sent_latent = halves(latent, first)
    dlatent, sent_dlatent = halves(dlatent, first)
    got = mate(jnp.concatenate([sent_latent, sent_dlatent], axis=1))

    def tokens_of(own, far):
        return jnp.concatenate([own, far], axis=0)

    grads = tokens_of(grad, far_grad)
    own = jnp.concatenate([halves(act, first)[0]] + [ours for ours, theirs in split], axis=1)
    far = jnp.concatenate([halves(far_act, first)[0]] + far_halves, axis=1)
    grad_butterfly = inner_rows(tokens_of(own, far), grads) * factor
    grad_butterfly = grad_butterfly.reshape(1, levels + 1, side // 2, side)
    grad_low_u = inner_rows(tokens_of(act, far_act), tokens_of(dlatent, got[:, rank // 2 :])) * factor
    grad_low_v = inner_rows(tokens_of(latent, got[:, : rank // 2]), grads) * factor
    return (output, grad_pre, grad_butterfly, grad_low_u, grad_low_v)


def solution(mesh):
    in_specs = (
        P(("hid", "seq"), None),
        P("hid", None, None, None),
        P("hid", None),
        P(None, "hid"),
        P(("hid", "seq"), None),
    )
    out_specs = (
        P(("hid", "seq"), None),
        P(("hid", "seq"), None),
        P("hid", None, "seq", None),
        P("hid", "seq"),
        P("seq", "hid"),
    )
    return jax.shard_map(
        on_device, mesh=mesh, in_specs=in_specs, out_specs=out_specs, check_vma=False
    )
```

```python
import math

import jax
import jax.numpy as jnp
from jax import lax
from jax.sharding import PartitionSpec as P


def exchange(x, mask):
    return lax.ppermute(x, "hid", [(i, i ^ mask) for i in range(lax.axis_size("hid"))])


def mate(x):
    return lax.ppermute(x, "seq", [(0, 1), (1, 0)])


def gelu_tanh(value):
    return jax.nn.gelu(value, approximate=True)


def dot(left, right):
    return jnp.dot(left, right, preferred_element_type=jnp.float32)


def dot_t(left, right):
    return lax.dot_general(
        left, right, (((1,), (1,)), ((), ())), preferred_element_type=jnp.float32
    )


def inner_rows(left, right):
    return lax.dot_general(
        left, right, (((0,), (0,)), ((), ())), preferred_element_type=jnp.float32
    )


def sum_over_hid(part, blocks):
    bits = (lax.axis_size("hid") - 1).bit_length()
    rounds = [(1, 2, 3)] + [(1 << bit,) for bit in range(2, bits)]
    total = part
    for at, masks in enumerate(rounds):
        sent = total.astype(jnp.bfloat16)
        if at == 1:
            late = {mask: blocks[mask] for mask in blocks if mask not in early}
            sent, late = lax.optimization_barrier((sent, late))
        got = [exchange(sent, mask) for mask in masks]
        if at == 0:
            early = {mask: exchange(blocks[mask], mask) for mask in blocks if mask not in masks}
            got = lax.optimization_barrier(got)
        elif at == 1:
            late = {mask: exchange(late[mask], mask) for mask in late}
            got, early = lax.optimization_barrier((got, early))
        else:
            got = lax.optimization_barrier(got)
        total = total + sum(x.astype(jnp.float32) for x in got)
    return total.astype(jnp.bfloat16), [(early | late)[mask] for mask in blocks]


def halves(x, first):
    width = x.shape[1] // 2
    low, high = x[:, :width], x[:, width:]
    return jnp.where(first, low, high), jnp.where(first, high, low)


def on_device(pre_act, butterfly, low_u, low_v, grad_out):
    tokens = pre_act.shape[0]
    hid = lax.axis_size("hid")
    first = lax.axis_index("seq") == 0
    side = butterfly.shape[-1]
    levels = butterfly.shape[1] - 1
    rank = low_u.shape[1]
    factor = 1.0 / math.sqrt(tokens * hid * lax.axis_size("seq"))

    pre_act, grad_out, first = lax.optimization_barrier((pre_act, grad_out, first))
    both = jnp.concatenate(
        [pre_act.reshape(tokens, hid, side), grad_out.reshape(tokens, hid, side)], axis=2
    ).reshape(tokens, hid * 2 * side)
    rows = lax.all_to_all(both, "hid", split_axis=1, concat_axis=0, tiled=True)
    pre_f = rows[:, :side].astype(jnp.float32)
    grad = rows[:, side:]
    act_f, pullback = jax.vjp(gelu_tanh, pre_f)
    act = act_f.astype(jnp.bfloat16)

    part = jnp.concatenate([dot(act, low_u), dot_t(grad, low_v)], axis=1)
    blocks = {}
    for level in range(1, levels + 1):
        term = dot_t(grad, butterfly[0, level]).astype(jnp.bfloat16)
        blocks[1 << level - 1] = jnp.concatenate([act, term], axis=1)
    latents, fars = sum_over_hid(part, blocks)
    latent, dlatent = latents[:, :rank], latents[:, rank:]

    acts = [act] + [far[:, :side] for far in fars]
    total = dot(act, butterfly[0, 0])
    back = dot_t(grad, butterfly[0, 0])
    for level in range(1, levels + 1):
        total = total + dot(acts[level], butterfly[0, level])
        back = back + fars[level - 1][:, side:].astype(jnp.float32)

    output_rows = (total + dot(latent, low_v)).astype(jnp.bfloat16)
    grad_act = (back + dot_t(dlatent, low_u)).astype(jnp.bfloat16)
    grad_pre_rows = pullback(grad_act.astype(jnp.float32))[0].astype(jnp.bfloat16)
    results = jnp.concatenate([output_rows, grad_pre_rows], axis=1)
    results = lax.all_to_all(results, "hid", split_axis=0, concat_axis=1, tiled=True)
    results = results.reshape(tokens, hid, 2 * side)
    output = results[:, :, :side].reshape(tokens, hid * side)
    grad_pre = results[:, :, side:].reshape(tokens, hid * side)

    split = [halves(x, first) for x in acts[1:]]
    got = mate(jnp.concatenate([grad, act] + [theirs for ours, theirs in split[::-1]], axis=1))
    far_grad, far_act = got[:, :side], got[:, side : 2 * side]
    far_halves = jnp.split(got[:, 2 * side :], levels, axis=1)[::-1]
    latent, sent_latent = halves(latent, first)
    dlatent, sent_dlatent = halves(dlatent, first)
    got = mate(jnp.concatenate([sent_latent, sent_dlatent], axis=1))

    def tokens_of(own, far):
        return jnp.concatenate([own, far], axis=0)

    grads = tokens_of(grad, far_grad)
    own = jnp.concatenate([halves(act, first)[0]] + [ours for ours, theirs in split], axis=1)
    far = jnp.concatenate([halves(far_act, first)[0]] + far_halves, axis=1)
    grad_butterfly = inner_rows(tokens_of(own, far), grads) * factor
    grad_butterfly = grad_butterfly.reshape(1, levels + 1, side // 2, side)
    grad_low_u = inner_rows(tokens_of(act, far_act), tokens_of(dlatent, got[:, rank // 2 :])) * factor
    grad_low_v = inner_rows(tokens_of(latent, got[:, : rank // 2]), grads) * factor
    return (output, grad_pre, grad_butterfly, grad_low_u, grad_low_v)


def solution(mesh):
    in_specs = (
        P(("hid", "seq"), None),
        P("hid", None, None, None),
        P("hid", None),
        P(None, "hid"),
        P(("hid", "seq"), None),
    )
    out_specs = (
        P(("hid", "seq"), None),
        P(("hid", "seq"), None),
        P("hid", None, "seq", None),
        P("hid", "seq"),
        P("seq", "hid"),
    )
    return jax.shard_map(
        on_device, mesh=mesh, in_specs=in_specs, out_specs=out_specs, check_vma=False
    )
```

```python
import math

import jax
import jax.numpy as jnp
from jax import lax
from jax.sharding import PartitionSpec as P


def exchange(x, mask):
    return lax.ppermute(x, "hid", [(i, i ^ mask) for i in range(lax.axis_size("hid"))])


def mate(x):
    return lax.ppermute(x, "seq", [(0, 1), (1, 0)])


def gelu_tanh(value):
    return jax.nn.gelu(value, approximate=True)


def dot(left, right):
    return jnp.dot(left, right, preferred_element_type=jnp.float32)


def dot_t(left, right):
    return lax.dot_general(
        left, right, (((1,), (1,)), ((), ())), preferred_element_type=jnp.float32
    )


def inner_rows(left, right):
    return lax.dot_general(
        left, right, (((0,), (0,)), ((), ())), preferred_element_type=jnp.float32
    )


def sum_over_hid(part, blocks, data):
    bits = (lax.axis_size("hid") - 1).bit_length()
    rounds = [(1, 2, 3)] + [(1 << bit,) for bit in range(2, bits)]
    total, far = part, {}
    for at, masks in enumerate(rounds):
        sent = total.astype(jnp.bfloat16)
        if at == 0:
            beside = {mask: blocks[mask] for mask in sorted(blocks, reverse=True) if mask > 3}
        elif at == 1:
            early, beside = far, {mask: blocks[mask] for mask in blocks if mask not in far}
            sent, beside = lax.optimization_barrier((sent, beside))
        else:
            beside = {}
        if at == len(rounds) - 1:
            sent, data = lax.optimization_barrier((sent, data))
        got = [exchange(sent, mask) for mask in masks]
        far = far | {mask: exchange(beside[mask], mask) for mask in beside}
        if at == 1:
            got, early = lax.optimization_barrier((got, early))
            far = far | early
        else:
            got = lax.optimization_barrier(got)
        total = total + sum(x.astype(jnp.float32) for x in got)
    return total.astype(jnp.bfloat16), [far[mask] for mask in blocks], data


def halves(x, first):
    width = x.shape[1] // 2
    low, high = x[:, :width], x[:, width:]
    return jnp.where(first, low, high), jnp.where(first, high, low)


def on_device(pre_act, butterfly, low_u, low_v, grad_out):
    tokens = pre_act.shape[0]
    hid = lax.axis_size("hid")
    first = lax.axis_index("seq") == 0
    side = butterfly.shape[-1]
    levels = butterfly.shape[1] - 1
    rank = low_u.shape[1]
    factor = 1.0 / math.sqrt(tokens * hid * lax.axis_size("seq"))

    pre_act, grad_out, first = lax.optimization_barrier((pre_act, grad_out, first))
    both = jnp.concatenate(
        [pre_act.reshape(tokens, hid, side), grad_out.reshape(tokens, hid, side)], axis=2
    ).reshape(tokens, hid * 2 * side)
    rows = lax.all_to_all(both, "hid", split_axis=1, concat_axis=0, tiled=True)
    pre_f = rows[:, :side].astype(jnp.float32)
    grad = rows[:, side:]
    act_f, pullback = jax.vjp(gelu_tanh, pre_f)
    act = act_f.astype(jnp.bfloat16)

    part = jnp.concatenate([dot(act, low_u), dot_t(grad, low_v)], axis=1)
    terms = dot_t(grad, butterfly.reshape((levels + 1) * side, side))
    back, *terms = jnp.split(terms, levels + 1, axis=1)
    blocks = {
        1 << level: jnp.concatenate([act, term.astype(jnp.bfloat16)], axis=1)
        for level, term in enumerate(terms)
    }
    latents, fars, (act, grad) = sum_over_hid(part, blocks, (act, grad))
    latent, dlatent = latents[:, :rank], latents[:, rank:]

    acts = [act] + [far[:, :side] for far in fars]
    total = dot(act, butterfly[0, 0])
    for level in range(1, levels + 1):
        total = total + dot(acts[level], butterfly[0, level])
        back = back + fars[level - 1][:, side:].astype(jnp.float32)

    output_rows = (total + dot(latent, low_v)).astype(jnp.bfloat16)
    grad_act = (back + dot_t(dlatent, low_u)).astype(jnp.bfloat16)
    grad_pre_rows = pullback(grad_act.astype(jnp.float32))[0].astype(jnp.bfloat16)
    results = jnp.concatenate([output_rows, grad_pre_rows], axis=1)
    results = lax.all_to_all(results, "hid", split_axis=0, concat_axis=1, tiled=True)
    results = results.reshape(tokens, hid, 2 * side)
    output = results[:, :, :side].reshape(tokens, hid * side)
    grad_pre = results[:, :, side:].reshape(tokens, hid * side)

    split = [halves(x, first) for x in acts[1:]]
    got = mate(jnp.concatenate([grad, act] + [theirs for ours, theirs in split[::-1]], axis=1))
    far_grad, far_act = got[:, :side], got[:, side : 2 * side]
    far_halves = jnp.split(got[:, 2 * side :], levels, axis=1)[::-1]
    latent, sent_latent = halves(latent, first)
    dlatent, sent_dlatent = halves(dlatent, first)
    got = mate(jnp.concatenate([sent_latent, sent_dlatent], axis=1))

    def tokens_of(own, far):
        return jnp.concatenate([own, far], axis=0)

    grads = tokens_of(grad, far_grad)
    own = jnp.concatenate([halves(act, first)[0]] + [ours for ours, theirs in split], axis=1)
    far = jnp.concatenate([halves(far_act, first)[0]] + far_halves, axis=1)
    grad_butterfly = inner_rows(tokens_of(own, far), grads) * factor
    grad_butterfly = grad_butterfly.reshape(1, levels + 1, side // 2, side)
    grad_low_u = inner_rows(tokens_of(act, far_act), tokens_of(dlatent, got[:, rank // 2 :])) * factor
    grad_low_v = inner_rows(tokens_of(latent, got[:, : rank // 2]), grads) * factor
    return (output, grad_pre, grad_butterfly, grad_low_u, grad_low_v)


def solution(mesh):
    in_specs = (
        P(("hid", "seq"), None),
        P("hid", None, None, None),
        P("hid", None),
        P(None, "hid"),
        P(("hid", "seq"), None),
    )
    out_specs = (
        P(("hid", "seq"), None),
        P(("hid", "seq"), None),
        P("hid", None, "seq", None),
        P("hid", "seq"),
        P("seq", "hid"),
    )
    return jax.shard_map(
        on_device, mesh=mesh, in_specs=in_specs, out_specs=out_specs, check_vma=False
    )
```

```python
import math

import jax
import jax.numpy as jnp
from jax import lax
from jax.sharding import PartitionSpec as P


def exchange(x, mask):
    return lax.ppermute(x, "hid", [(i, i ^ mask) for i in range(lax.axis_size("hid"))])


def mate(x):
    return lax.ppermute(x, "seq", [(0, 1), (1, 0)])


def gelu_tanh(value):
    return jax.nn.gelu(value, approximate=True)


def dot(left, right):
    return jnp.dot(left, right, preferred_element_type=jnp.float32)


def dot_t(left, right):
    return lax.dot_general(
        left, right, (((1,), (1,)), ((), ())), preferred_element_type=jnp.float32
    )


def inner_rows(left, right):
    return lax.dot_general(
        left, right, (((0,), (0,)), ((), ())), preferred_element_type=jnp.float32
    )


def sum_over_hid(part, blocks, data):
    bits = (lax.axis_size("hid") - 1).bit_length()
    rounds = [(1, 2, 3)] + [(1 << bit,) for bit in range(2, bits)]
    total, far = part, {}
    for at, masks in enumerate(rounds):
        sent = total.astype(jnp.bfloat16)
        if at == 0:
            beside = {mask: blocks[mask] for mask in sorted(blocks, reverse=True) if mask > 3}
        elif at == 1:
            early, beside = far, {mask: blocks[mask] for mask in blocks if mask not in far}
            sent, beside = lax.optimization_barrier((sent, beside))
        else:
            beside = {}
        if at == len(rounds) - 1:
            sent, data = lax.optimization_barrier((sent, data))
        got = [exchange(sent, mask) for mask in masks]
        far = far | {mask: exchange(beside[mask], mask) for mask in beside}
        if at == 1:
            got, early = lax.optimization_barrier((got, early))
            far = far | early
        else:
            got = lax.optimization_barrier(got)
        total = total + sum(x.astype(jnp.float32) for x in got)
    return total.astype(jnp.bfloat16), [far[mask] for mask in blocks], data


def halves(x, first):
    width = x.shape[1] // 2
    low, high = x[:, :width], x[:, width:]
    return jnp.where(first, low, high), jnp.where(first, high, low)


def on_device(pre_act, butterfly, low_u, low_v, grad_out):
    tokens = pre_act.shape[0]
    hid = lax.axis_size("hid")
    first = lax.axis_index("seq") == 0
    side = butterfly.shape[-1]
    levels = butterfly.shape[1] - 1
    rank = low_u.shape[1]
    factor = 1.0 / math.sqrt(tokens * hid * lax.axis_size("seq"))

    pre_act, grad_out, first = lax.optimization_barrier((pre_act, grad_out, first))
    both = jnp.concatenate(
        [pre_act.reshape(tokens, hid, side), grad_out.reshape(tokens, hid, side)], axis=2
    ).reshape(tokens, hid * 2 * side)
    rows = lax.all_to_all(both, "hid", split_axis=1, concat_axis=0, tiled=True)
    pre_f = rows[:, :side].astype(jnp.float32)
    grad = rows[:, side:]
    act_f, pullback = jax.vjp(gelu_tanh, pre_f)
    act = act_f.astype(jnp.bfloat16)

    part = jnp.concatenate([dot(act, low_u), dot_t(grad, low_v)], axis=1)
    terms = dot_t(grad, butterfly.reshape((levels + 1) * side, side))
    back, *terms = jnp.split(terms, levels + 1, axis=1)
    blocks = {
        1 << level: jnp.concatenate([act, term.astype(jnp.bfloat16)], axis=1)
        for level, term in enumerate(terms)
    }
    latents, fars, (act, grad) = sum_over_hid(part, blocks, (act, grad))
    latent, dlatent = latents[:, :rank], latents[:, rank:]

    acts = [act] + [far[:, :side] for far in fars]
    total = dot(act, butterfly[0, 0])
    for level in range(1, levels + 1):
        total = total + dot(acts[level], butterfly[0, level])
        back = back + fars[level - 1][:, side:].astype(jnp.float32)

    output_rows = (total + dot(latent, low_v)).astype(jnp.bfloat16)
    grad_act = (back + dot_t(dlatent, low_u)).astype(jnp.bfloat16)
    grad_pre_rows = pullback(grad_act.astype(jnp.float32))[0].astype(jnp.bfloat16)
    results = jnp.concatenate([output_rows, grad_pre_rows], axis=1)
    split = [halves(x, first) for x in acts[1:]]
    latent, sent_latent = halves(latent, first)
    dlatent, sent_dlatent = halves(dlatent, first)
    sent = [grad, act, sent_latent, sent_dlatent] + [theirs for ours, theirs in split]
    results, sent = lax.optimization_barrier((results, jnp.concatenate(sent, axis=1)))
    results = lax.all_to_all(results.reshape(hid, tokens, 2 * side), "hid", 0, 0, tiled=True)

    got = mate(sent)
    ends = [side, 2 * side, 2 * side + rank // 2, 2 * side + rank]
    far_grad, far_act, far_latent, far_dlatent, far_halves = jnp.split(got, ends, axis=1)

    def tokens_of(own, far):
        return jnp.concatenate([own, far], axis=0)

    grads = tokens_of(grad, far_grad)
    own = jnp.concatenate([halves(act, first)[0]] + [ours for ours, theirs in split], axis=1)
    far = jnp.concatenate([halves(far_act, first)[0], far_halves], axis=1)
    grad_butterfly = inner_rows(tokens_of(own, far), grads) * factor
    grad_butterfly = grad_butterfly.reshape(1, levels + 1, side // 2, side)
    grad_low_u = inner_rows(tokens_of(act, far_act), tokens_of(dlatent, far_dlatent)) * factor
    grad_low_v = inner_rows(tokens_of(latent, far_latent), grads) * factor

    results, grad_butterfly, grad_low_u, grad_low_v = lax.optimization_barrier(
        (results, grad_butterfly, grad_low_u, grad_low_v)
    )
    output = results[:, :, :side].transpose(1, 0, 2).reshape(tokens, hid * side)
    grad_pre = results[:, :, side:].transpose(1, 0, 2).reshape(tokens, hid * side)
    return (output, grad_pre, grad_butterfly, grad_low_u, grad_low_v)


def solution(mesh):
    in_specs = (
        P(("hid", "seq"), None),
        P("hid", None, None, None),
        P("hid", None),
        P(None, "hid"),
        P(("hid", "seq"), None),
    )
    out_specs = (
        P(("hid", "seq"), None),
        P(("hid", "seq"), None),
        P("hid", None, "seq", None),
        P("hid", "seq"),
        P("seq", "hid"),
    )
    return jax.shard_map(
        on_device, mesh=mesh, in_specs=in_specs, out_specs=out_specs, check_vma=False
    )
```

```python
import math

import jax
import jax.numpy as jnp
from jax import lax
from jax.sharding import PartitionSpec as P


def exchange(x, mask):
    return lax.ppermute(x, "hid", [(i, i ^ mask) for i in range(lax.axis_size("hid"))])


def mate(x):
    return lax.ppermute(x, "seq", [(0, 1), (1, 0)])


def gelu_tanh(value):
    return jax.nn.gelu(value, approximate=True)


def dot(left, right):
    return jnp.dot(left, right, preferred_element_type=jnp.float32)


def dot_t(left, right):
    return lax.dot_general(
        left, right, (((1,), (1,)), ((), ())), preferred_element_type=jnp.float32
    )


def inner_rows(left, right):
    return lax.dot_general(
        left, right, (((0,), (0,)), ((), ())), preferred_element_type=jnp.float32
    )


def sum_over_hid(part, blocks, data):
    bits = (lax.axis_size("hid") - 1).bit_length()
    rounds = [(1, 2, 3)] + [(1 << bit,) for bit in range(2, bits)]
    total, far = part, {}
    for at, masks in enumerate(rounds):
        sent = total.astype(jnp.bfloat16)
        if at == 0:
            beside = {mask: blocks[mask] for mask in sorted(blocks, reverse=True) if mask > 3}
        elif at == 1:
            early, beside = far, {mask: blocks[mask] for mask in blocks if mask not in far}
            sent, beside = lax.optimization_barrier((sent, beside))
        else:
            beside = {}
        if at == len(rounds) - 1:
            sent, data = lax.optimization_barrier((sent, data))
        got = [exchange(sent, mask) for mask in masks]
        far = far | {mask: exchange(beside[mask], mask) for mask in beside}
        if at == 1:
            got, early = lax.optimization_barrier((got, early))
            far = far | early
        else:
            got = lax.optimization_barrier(got)
        total = total + sum(x.astype(jnp.float32) for x in got)
    return total.astype(jnp.bfloat16), [far[mask] for mask in blocks], data


def halves(x, first):
    width = x.shape[1] // 2
    low, high = x[:, :width], x[:, width:]
    return jnp.where(first, low, high), jnp.where(first, high, low)


def on_device(pre_act, butterfly, low_u, low_v, grad_out):
    tokens = pre_act.shape[0]
    hid = lax.axis_size("hid")
    first = lax.axis_index("seq") == 0
    side = butterfly.shape[-1]
    levels = butterfly.shape[1] - 1
    rank = low_u.shape[1]
    factor = 1.0 / math.sqrt(tokens * hid * lax.axis_size("seq"))

    pre_act, grad_out, first = lax.optimization_barrier((pre_act, grad_out, first))
    both = jnp.concatenate(
        [pre_act.reshape(tokens, hid, side), grad_out.reshape(tokens, hid, side)], axis=2
    ).reshape(tokens, hid * 2 * side)
    rows = lax.all_to_all(both, "hid", split_axis=1, concat_axis=0, tiled=True)
    pre_f = rows[:, :side].astype(jnp.float32)
    grad = rows[:, side:]
    act_f, pullback = jax.vjp(gelu_tanh, pre_f)
    act = act_f.astype(jnp.bfloat16)

    part = jnp.concatenate([dot(act, low_u), dot_t(grad, low_v)], axis=1)
    terms = dot_t(grad, butterfly.reshape((levels + 1) * side, side))
    back, *terms = jnp.split(terms, levels + 1, axis=1)
    blocks = {
        1 << level: jnp.concatenate([act, term.astype(jnp.bfloat16)], axis=1)
        for level, term in enumerate(terms)
    }
    latents, fars, (act, grad) = sum_over_hid(part, blocks, (act, grad))
    latent, dlatent = latents[:, :rank], latents[:, rank:]

    acts = [act] + [far[:, :side] for far in fars]
    total = dot(act, butterfly[0, 0])
    for level in range(1, levels + 1):
        total = total + dot(acts[level], butterfly[0, level])
        back = back + fars[level - 1][:, side:].astype(jnp.float32)

    output_rows = (total + dot(latent, low_v)).astype(jnp.bfloat16)
    grad_act = (back + dot_t(dlatent, low_u)).astype(jnp.bfloat16)
    grad_pre_rows = pullback(grad_act.astype(jnp.float32))[0].astype(jnp.bfloat16)
    results = jnp.concatenate([output_rows, grad_pre_rows], axis=1)
    split = [halves(x, first) for x in acts[1:]]
    latent, sent_latent = halves(latent, first)
    dlatent, sent_dlatent = halves(dlatent, first)
    sent = [grad, act, sent_latent, sent_dlatent] + [theirs for ours, theirs in split]
    results = results.reshape(hid, tokens, 2 * side)
    results, sent = lax.optimization_barrier((results, sent))
    results = lax.all_to_all(results, "hid", 0, 0, tiled=True)

    got = mate(jnp.concatenate(sent, axis=1))
    ends = [side, 2 * side, 2 * side + rank // 2, 2 * side + rank]
    far_grad, far_act, far_latent, far_dlatent, far_halves = jnp.split(got, ends, axis=1)

    def tokens_of(own, far):
        return jnp.concatenate([own, far], axis=0)

    grads = tokens_of(grad, far_grad)
    own = jnp.concatenate([halves(act, first)[0]] + [ours for ours, theirs in split], axis=1)
    far = jnp.concatenate([halves(far_act, first)[0], far_halves], axis=1)
    grad_butterfly = inner_rows(tokens_of(own, far), grads) * factor
    grad_butterfly = grad_butterfly.reshape(1, levels + 1, side // 2, side)
    grad_low_u = inner_rows(tokens_of(act, far_act), tokens_of(dlatent, far_dlatent)) * factor
    grad_low_v = inner_rows(tokens_of(latent, far_latent), grads) * factor

    results, grad_butterfly, grad_low_u, grad_low_v = lax.optimization_barrier(
        (results, grad_butterfly, grad_low_u, grad_low_v)
    )
    output = results[:, :, :side].transpose(1, 0, 2).reshape(tokens, hid * side)
    grad_pre = results[:, :, side:].transpose(1, 0, 2).reshape(tokens, hid * side)
    return (output, grad_pre, grad_butterfly, grad_low_u, grad_low_v)


def solution(mesh):
    in_specs = (
        P(("hid", "seq"), None),
        P("hid", None, None, None),
        P("hid", None),
        P(None, "hid"),
        P(("hid", "seq"), None),
    )
    out_specs = (
        P(("hid", "seq"), None),
        P(("hid", "seq"), None),
        P("hid", None, "seq", None),
        P("hid", "seq"),
        P("seq", "hid"),
    )
    return jax.shard_map(
        on_device, mesh=mesh, in_specs=in_specs, out_specs=out_specs, check_vma=False
    )
```

```python
import math

import jax
import jax.numpy as jnp
from jax import lax
from jax.sharding import PartitionSpec as P


def exchange(x, mask):
    return lax.ppermute(x, "hid", [(i, i ^ mask) for i in range(lax.axis_size("hid"))])


def mate(x):
    return lax.ppermute(x, "seq", [(0, 1), (1, 0)])


def gelu_tanh(value):
    return jax.nn.gelu(value, approximate=True)


def dot(left, right):
    return jnp.dot(left, right, preferred_element_type=jnp.float32)


def dot_t(left, right):
    return lax.dot_general(
        left, right, (((1,), (1,)), ((), ())), preferred_element_type=jnp.float32
    )


def inner_rows(left, right):
    return lax.dot_general(
        left, right, (((0,), (0,)), ((), ())), preferred_element_type=jnp.float32
    )


def sum_over_hid(part, blocks, data):
    bits = (lax.axis_size("hid") - 1).bit_length()
    rounds = [(1, 2, 3)] + [(1 << bit,) for bit in range(2, bits)]
    total, far = part, {}
    for at, masks in enumerate(rounds):
        sent = total.astype(jnp.bfloat16)
        if at == 0:
            beside = {mask: blocks[mask] for mask in sorted(blocks, reverse=True) if mask > 3}
        elif at == 1:
            early, beside = far, {mask: blocks[mask] for mask in blocks if mask not in far}
            sent, beside = lax.optimization_barrier((sent, beside))
        else:
            beside = {}
        if at == len(rounds) - 1:
            sent, data = lax.optimization_barrier((sent, data))
        got = [exchange(sent, mask) for mask in masks]
        far = far | {mask: exchange(beside[mask], mask) for mask in beside}
        if at == 1:
            got, early = lax.optimization_barrier((got, early))
            far = far | early
        else:
            got = lax.optimization_barrier(got)
        total = total + sum(x.astype(jnp.float32) for x in got)
    return total.astype(jnp.bfloat16), [far[mask] for mask in blocks], data


def halves(x, first):
    width = x.shape[1] // 2
    low, high = x[:, :width], x[:, width:]
    return jnp.where(first, low, high), jnp.where(first, high, low)


def on_device(pre_act, butterfly, low_u, low_v, grad_out):
    tokens = pre_act.shape[0]
    hid = lax.axis_size("hid")
    first = lax.axis_index("seq") == 0
    side = butterfly.shape[-1]
    levels = butterfly.shape[1] - 1
    rank = low_u.shape[1]
    factor = 1.0 / math.sqrt(tokens * hid * lax.axis_size("seq"))

    pre_act, grad_out, first = lax.optimization_barrier((pre_act, grad_out, first))
    both = jnp.concatenate(
        [pre_act.reshape(tokens, hid, side), grad_out.reshape(tokens, hid, side)], axis=2
    ).reshape(tokens, hid * 2 * side)
    rows = lax.all_to_all(both, "hid", split_axis=1, concat_axis=0, tiled=True)
    pre_f = rows[:, :side].astype(jnp.float32)
    grad = rows[:, side:]
    act_f, pullback = jax.vjp(gelu_tanh, pre_f)
    act = act_f.astype(jnp.bfloat16)

    part = jnp.concatenate([dot(act, low_u), dot_t(grad, low_v)], axis=1)
    terms = dot_t(grad, butterfly.reshape((levels + 1) * side, side))
    back, *terms = jnp.split(terms, levels + 1, axis=1)
    blocks = {
        1 << level: jnp.concatenate([act, term.astype(jnp.bfloat16)], axis=1)
        for level, term in enumerate(terms)
    }
    latents, fars, (act, grad) = sum_over_hid(part, blocks, (act, grad))
    latent, dlatent = latents[:, :rank], latents[:, rank:]

    acts = [act] + [far[:, :side] for far in fars]
    total = dot(act, butterfly[0, 0])
    for level in range(1, levels + 1):
        total = total + dot(acts[level], butterfly[0, level])
        back = back + fars[level - 1][:, side:].astype(jnp.float32)

    output_rows = (total + dot(latent, low_v)).astype(jnp.bfloat16)
    grad_act = (back + dot_t(dlatent, low_u)).astype(jnp.bfloat16)
    grad_pre_rows = pullback(grad_act.astype(jnp.float32))[0].astype(jnp.bfloat16)
    results = jnp.concatenate([output_rows, grad_pre_rows], axis=1)
    results = lax.all_to_all(results, "hid", split_axis=0, concat_axis=1, tiled=True)
    results = results.reshape(tokens, hid, 2 * side)
    output = results[:, :, :side].reshape(tokens, hid * side)
    grad_pre = results[:, :, side:].reshape(tokens, hid * side)

    split = [halves(x, first) for x in acts[1:]]
    got = mate(jnp.concatenate([grad, act] + [theirs for ours, theirs in split[::-1]], axis=1))
    far_grad, far_act = got[:, :side], got[:, side : 2 * side]
    far_halves = jnp.split(got[:, 2 * side :], levels, axis=1)[::-1]
    latent, sent_latent = halves(latent, first)
    dlatent, sent_dlatent = halves(dlatent, first)
    got = mate(jnp.concatenate([sent_latent, sent_dlatent], axis=1))

    def tokens_of(own, far):
        return jnp.concatenate([own, far], axis=0)

    grads = tokens_of(grad, far_grad)
    own = jnp.concatenate([halves(act, first)[0]] + [ours for ours, theirs in split], axis=1)
    far = jnp.concatenate([halves(far_act, first)[0]] + far_halves, axis=1)
    grad_butterfly = inner_rows(tokens_of(own, far), grads) * factor
    grad_butterfly = grad_butterfly.reshape(1, levels + 1, side // 2, side)
    got, grad_butterfly = lax.optimization_barrier((got, grad_butterfly))
    grad_low_u = inner_rows(tokens_of(act, far_act), tokens_of(dlatent, got[:, rank // 2 :])) * factor
    grad_low_v = inner_rows(tokens_of(latent, got[:, : rank // 2]), grads) * factor
    return (output, grad_pre, grad_butterfly, grad_low_u, grad_low_v)


def solution(mesh):
    in_specs = (
        P(("hid", "seq"), None),
        P("hid", None, None, None),
        P("hid", None),
        P(None, "hid"),
        P(("hid", "seq"), None),
    )
    out_specs = (
        P(("hid", "seq"), None),
        P(("hid", "seq"), None),
        P("hid", None, "seq", None),
        P("hid", "seq"),
        P("seq", "hid"),
    )
    return jax.shard_map(
        on_device, mesh=mesh, in_specs=in_specs, out_specs=out_specs, check_vma=False
    )
```

```python
import math

import jax
import jax.numpy as jnp
from jax import lax
from jax.sharding import PartitionSpec as P


def exchange(x, mask):
    return lax.ppermute(x, "hid", [(i, i ^ mask) for i in range(lax.axis_size("hid"))])


def mate(x):
    return lax.ppermute(x, "seq", [(0, 1), (1, 0)])


def gelu_tanh(value):
    return jax.nn.gelu(value, approximate=True)


def dot(left, right):
    return jnp.dot(left, right, preferred_element_type=jnp.float32)


def dot_t(left, right):
    return lax.dot_general(
        left, right, (((1,), (1,)), ((), ())), preferred_element_type=jnp.float32
    )


def inner_rows(left, right):
    return lax.dot_general(
        left, right, (((0,), (0,)), ((), ())), preferred_element_type=jnp.float32
    )


def sum_over_hid(part, blocks, data):
    bits = (lax.axis_size("hid") - 1).bit_length()
    rounds = [(1, 2, 3)] + [(1 << bit,) for bit in range(2, bits)]
    total, far = part, {}
    for at, masks in enumerate(rounds):
        sent = total.astype(jnp.bfloat16)
        if at == 0:
            beside = {max(blocks): blocks[max(blocks)]}
        elif at == 1:
            early, beside = far, {mask: blocks[mask] for mask in rounds[0] if mask in blocks}
        elif at == len(rounds) - 1:
            early, beside = {}, {mask: blocks[mask] for mask in blocks if mask not in far}
            sent, data = lax.optimization_barrier((sent, data))
        else:
            early, beside = {}, {}
        if at:
            sent, beside = lax.optimization_barrier((sent, beside))
        got = [exchange(sent, mask) for mask in masks]
        moved = {mask: exchange(beside[mask], mask) for mask in beside}
        if at == 0:
            got = lax.optimization_barrier(got)
        elif at == len(rounds) - 1:
            got, moved = lax.optimization_barrier((got, moved))
        else:
            got, early = lax.optimization_barrier((got, early))
            far = far | early
        far = far | moved
        total = total + sum(x.astype(jnp.float32) for x in got)
    return total.astype(jnp.bfloat16), [far[mask] for mask in blocks], data


def halves(x, first):
    width = x.shape[1] // 2
    low, high = x[:, :width], x[:, width:]
    return jnp.where(first, low, high), jnp.where(first, high, low)


def on_device(pre_act, butterfly, low_u, low_v, grad_out):
    tokens = pre_act.shape[0]
    hid = lax.axis_size("hid")
    first = lax.axis_index("seq") == 0
    side = butterfly.shape[-1]
    levels = butterfly.shape[1] - 1
    rank = low_u.shape[1]
    factor = 1.0 / math.sqrt(tokens * hid * lax.axis_size("seq"))

    pre_act, grad_out, first = lax.optimization_barrier((pre_act, grad_out, first))
    both = jnp.concatenate(
        [pre_act.reshape(tokens, hid, side), grad_out.reshape(tokens, hid, side)], axis=2
    ).reshape(tokens, hid * 2 * side)
    rows = lax.all_to_all(both, "hid", split_axis=1, concat_axis=0, tiled=True)
    pre_f = rows[:, :side].astype(jnp.float32)
    grad = rows[:, side:]
    act_f, pullback = jax.vjp(gelu_tanh, pre_f)
    act = act_f.astype(jnp.bfloat16)

    part = jnp.concatenate([dot(act, low_u), dot_t(grad, low_v)], axis=1)
    terms = dot_t(grad, butterfly.reshape((levels + 1) * side, side))
    back, *terms = jnp.split(terms, levels + 1, axis=1)
    blocks = {
        1 << level: jnp.concatenate([act, term.astype(jnp.bfloat16)], axis=1)
        for level, term in enumerate(terms)
    }
    latents, fars, (act, grad) = sum_over_hid(part, blocks, (act, grad))
    latent, dlatent = latents[:, :rank], latents[:, rank:]

    acts = [act] + [far[:, :side] for far in fars]
    total = dot(act, butterfly[0, 0])
    for level in range(1, levels + 1):
        total = total + dot(acts[level], butterfly[0, level])
        back = back + fars[level - 1][:, side:].astype(jnp.float32)

    output_rows = (total + dot(latent, low_v)).astype(jnp.bfloat16)
    grad_act = (back + dot_t(dlatent, low_u)).astype(jnp.bfloat16)
    grad_pre_rows = pullback(grad_act.astype(jnp.float32))[0].astype(jnp.bfloat16)
    results = jnp.concatenate([output_rows, grad_pre_rows], axis=1)
    results = lax.all_to_all(results, "hid", split_axis=0, concat_axis=1, tiled=True)
    results = results.reshape(tokens, hid, 2 * side)
    output = results[:, :, :side].reshape(tokens, hid * side)
    grad_pre = results[:, :, side:].reshape(tokens, hid * side)

    split = [halves(x, first) for x in acts[1:]]
    got = mate(jnp.concatenate([grad, act] + [theirs for ours, theirs in split[::-1]], axis=1))
    far_grad, far_act = got[:, :side], got[:, side : 2 * side]
    far_halves = jnp.split(got[:, 2 * side :], levels, axis=1)[::-1]
    latent, sent_latent = halves(latent, first)
    dlatent, sent_dlatent = halves(dlatent, first)
    got = mate(jnp.concatenate([sent_latent, sent_dlatent], axis=1))

    def tokens_of(own, far):
        return jnp.concatenate([own, far], axis=0)

    grads = tokens_of(grad, far_grad)
    own = jnp.concatenate([halves(act, first)[0]] + [ours for ours, theirs in split], axis=1)
    far = jnp.concatenate([halves(far_act, first)[0]] + far_halves, axis=1)
    grad_butterfly = inner_rows(tokens_of(own, far), grads) * factor
    grad_butterfly = grad_butterfly.reshape(1, levels + 1, side // 2, side)
    got, grad_butterfly = lax.optimization_barrier((got, grad_butterfly))
    grad_low_u = inner_rows(tokens_of(act, far_act), tokens_of(dlatent, got[:, rank // 2 :])) * factor
    grad_low_v = inner_rows(tokens_of(latent, got[:, : rank // 2]), grads) * factor
    return (output, grad_pre, grad_butterfly, grad_low_u, grad_low_v)


def solution(mesh):
    in_specs = (
        P(("hid", "seq"), None),
        P("hid", None, None, None),
        P("hid", None),
        P(None, "hid"),
        P(("hid", "seq"), None),
    )
    out_specs = (
        P(("hid", "seq"), None),
        P(("hid", "seq"), None),
        P("hid", None, "seq", None),
        P("hid", "seq"),
        P("seq", "hid"),
    )
    return jax.shard_map(
        on_device, mesh=mesh, in_specs=in_specs, out_specs=out_specs, check_vma=False
    )
```

```python
import math

import jax
import jax.numpy as jnp
from jax import lax
from jax.sharding import PartitionSpec as P


def exchange(x, mask):
    return lax.ppermute(x, "hid", [(i, i ^ mask) for i in range(lax.axis_size("hid"))])


def mate(x):
    return lax.ppermute(x, "seq", [(0, 1), (1, 0)])


def gelu_tanh(value):
    return jax.nn.gelu(value, approximate=True)


def dot(left, right):
    return jnp.dot(left, right, preferred_element_type=jnp.float32)


def dot_t(left, right):
    return lax.dot_general(
        left, right, (((1,), (1,)), ((), ())), preferred_element_type=jnp.float32
    )


def inner_rows(left, right):
    return lax.dot_general(
        left, right, (((0,), (0,)), ((), ())), preferred_element_type=jnp.float32
    )


def sum_over_hid(part, blocks, data):
    bits = (lax.axis_size("hid") - 1).bit_length()
    rounds = [(3, 1, 2)] + [(1 << bit,) for bit in range(2, bits)]
    total, far = part, {}
    for at, masks in enumerate(rounds):
        sent = total.astype(jnp.bfloat16)
        if at == 0:
            beside = {mask: blocks[mask] for mask in sorted(blocks, reverse=True) if mask > 3}
        elif at == 1:
            early, beside = far, {mask: blocks[mask] for mask in blocks if mask not in far}
            sent, beside = lax.optimization_barrier((sent, beside))
        else:
            beside = {}
        if at == len(rounds) - 1:
            sent, data = lax.optimization_barrier((sent, data))
        got = [exchange(sent, mask) for mask in masks]
        far = far | {mask: exchange(beside[mask], mask) for mask in beside}
        if at == 1:
            got, early = lax.optimization_barrier((got, early))
            far = far | early
        else:
            got = lax.optimization_barrier(got)
        total = total + sum(x.astype(jnp.float32) for x in got)
    return total.astype(jnp.bfloat16), [far[mask] for mask in blocks], data


def halves(x, first):
    width = x.shape[1] // 2
    low, high = x[:, :width], x[:, width:]
    return jnp.where(first, low, high), jnp.where(first, high, low)


def on_device(pre_act, butterfly, low_u, low_v, grad_out):
    tokens = pre_act.shape[0]
    hid = lax.axis_size("hid")
    first = lax.axis_index("seq") == 0
    side = butterfly.shape[-1]
    levels = butterfly.shape[1] - 1
    rank = low_u.shape[1]
    factor = 1.0 / math.sqrt(tokens * hid * lax.axis_size("seq"))

    pre_act, grad_out, first = lax.optimization_barrier((pre_act, grad_out, first))
    both = jnp.concatenate(
        [pre_act.reshape(tokens, hid, side), grad_out.reshape(tokens, hid, side)], axis=2
    ).reshape(tokens, hid * 2 * side)
    rows = lax.all_to_all(both, "hid", split_axis=1, concat_axis=0, tiled=True)
    pre_f = rows[:, :side].astype(jnp.float32)
    grad = rows[:, side:]
    act_f, pullback = jax.vjp(gelu_tanh, pre_f)
    act = act_f.astype(jnp.bfloat16)

    part = jnp.concatenate([dot(act, low_u), dot_t(grad, low_v)], axis=1)
    terms = dot_t(grad, butterfly.reshape((levels + 1) * side, side))
    back, *terms = jnp.split(terms, levels + 1, axis=1)
    blocks = {
        1 << level: jnp.concatenate([act, term.astype(jnp.bfloat16)], axis=1)
        for level, term in enumerate(terms)
    }
    latents, fars, (act, grad) = sum_over_hid(part, blocks, (act, grad))
    latent, dlatent = latents[:, :rank], latents[:, rank:]

    acts = [act] + [far[:, :side] for far in fars]
    total = dot(act, butterfly[0, 0])
    for level in range(1, levels + 1):
        total = total + dot(acts[level], butterfly[0, level])
        back = back + fars[level - 1][:, side:].astype(jnp.float32)

    output_rows = (total + dot(latent, low_v)).astype(jnp.bfloat16)
    grad_act = (back + dot_t(dlatent, low_u)).astype(jnp.bfloat16)
    grad_pre_rows = pullback(grad_act.astype(jnp.float32))[0].astype(jnp.bfloat16)
    results = jnp.concatenate([output_rows, grad_pre_rows], axis=1)
    results = lax.all_to_all(results, "hid", split_axis=0, concat_axis=1, tiled=True)
    results = results.reshape(tokens, hid, 2 * side)
    output = results[:, :, :side].reshape(tokens, hid * side)
    grad_pre = results[:, :, side:].reshape(tokens, hid * side)

    split = [halves(x, first) for x in acts[1:]]
    got = mate(jnp.concatenate([grad, act] + [theirs for ours, theirs in split[::-1]], axis=1))
    far_grad, far_act = got[:, :side], got[:, side : 2 * side]
    far_halves = jnp.split(got[:, 2 * side :], levels, axis=1)[::-1]
    latent, sent_latent = halves(latent, first)
    dlatent, sent_dlatent = halves(dlatent, first)
    got = mate(jnp.concatenate([sent_latent, sent_dlatent], axis=1))

    def tokens_of(own, far):
        return jnp.concatenate([own, far], axis=0)

    grads = tokens_of(grad, far_grad)
    own = jnp.concatenate([halves(act, first)[0]] + [ours for ours, theirs in split], axis=1)
    far = jnp.concatenate([halves(far_act, first)[0]] + far_halves, axis=1)
    grad_butterfly = inner_rows(tokens_of(own, far), grads) * factor
    grad_butterfly = grad_butterfly.reshape(1, levels + 1, side // 2, side)
    got, grad_butterfly = lax.optimization_barrier((got, grad_butterfly))
    grad_low_u = inner_rows(tokens_of(act, far_act), tokens_of(dlatent, got[:, rank // 2 :])) * factor
    grad_low_v = inner_rows(tokens_of(latent, got[:, : rank // 2]), grads) * factor
    return (output, grad_pre, grad_butterfly, grad_low_u, grad_low_v)


def solution(mesh):
    in_specs = (
        P(("hid", "seq"), None),
        P("hid", None, None, None),
        P("hid", None),
        P(None, "hid"),
        P(("hid", "seq"), None),
    )
    out_specs = (
        P(("hid", "seq"), None),
        P(("hid", "seq"), None),
        P("hid", None, "seq", None),
        P("hid", "seq"),
        P("seq", "hid"),
    )
    return jax.shard_map(
        on_device, mesh=mesh, in_specs=in_specs, out_specs=out_specs, check_vma=False
    )
```

```python
import math

import jax
import jax.numpy as jnp
from jax import lax
from jax.sharding import PartitionSpec as P


def exchange(x, mask):
    return lax.ppermute(x, "hid", [(i, i ^ mask) for i in range(lax.axis_size("hid"))])


def mate(x):
    return lax.ppermute(x, "seq", [(0, 1), (1, 0)])


def gelu_tanh(value):
    return jax.nn.gelu(value, approximate=True)


def dot(left, right):
    return jnp.dot(left, right, preferred_element_type=jnp.float32)


def dot_t(left, right):
    return lax.dot_general(
        left, right, (((1,), (1,)), ((), ())), preferred_element_type=jnp.float32
    )


def inner_rows(left, right):
    return lax.dot_general(
        left, right, (((0,), (0,)), ((), ())), preferred_element_type=jnp.float32
    )


def sum_over_hid(part, blocks, data):
    bits = (lax.axis_size("hid") - 1).bit_length()
    rounds = [(3, 1, 2)] + [(1 << bit,) for bit in range(2, bits)]
    total, far = part, {}
    for at, masks in enumerate(rounds):
        sent = total.astype(jnp.bfloat16)
        if at == 0:
            beside = {mask: blocks[mask] for mask in sorted(blocks, reverse=True) if mask > 3}
        elif at == 1:
            early, beside = far, {mask: blocks[mask] for mask in blocks if mask not in far}
            sent, beside = lax.optimization_barrier((sent, beside))
        else:
            beside = {}
        if at == len(rounds) - 1:
            sent, data = lax.optimization_barrier((sent, data))
        got = [exchange(sent, mask) for mask in masks]
        far = far | {mask: exchange(beside[mask], mask) for mask in beside}
        if at == 1:
            got, blocks_early = lax.optimization_barrier((got, list(early.values())))
            far = far | dict(zip(early, blocks_early))
        else:
            got = lax.optimization_barrier(got)
        total = total + sum(x.astype(jnp.float32) for x in got)
    return total.astype(jnp.bfloat16), [far[mask] for mask in blocks], data


def halves(x, first):
    width = x.shape[1] // 2
    low, high = x[:, :width], x[:, width:]
    return jnp.where(first, low, high), jnp.where(first, high, low)


def on_device(pre_act, butterfly, low_u, low_v, grad_out):
    tokens = pre_act.shape[0]
    hid = lax.axis_size("hid")
    first = lax.axis_index("seq") == 0
    side = butterfly.shape[-1]
    levels = butterfly.shape[1] - 1
    rank = low_u.shape[1]
    factor = 1.0 / math.sqrt(tokens * hid * lax.axis_size("seq"))

    pre_act, grad_out, first = lax.optimization_barrier((pre_act, grad_out, first))
    both = jnp.concatenate(
        [pre_act.reshape(tokens, hid, side), grad_out.reshape(tokens, hid, side)], axis=2
    ).reshape(tokens, hid * 2 * side)
    rows = lax.all_to_all(both, "hid", split_axis=1, concat_axis=0, tiled=True)
    pre_f = rows[:, :side].astype(jnp.float32)
    grad = rows[:, side:]
    act_f, pullback = jax.vjp(gelu_tanh, pre_f)
    act = act_f.astype(jnp.bfloat16)

    part = jnp.concatenate([dot(act, low_u), dot_t(grad, low_v)], axis=1)
    terms = dot_t(grad, butterfly.reshape((levels + 1) * side, side))
    back, *terms = jnp.split(terms, levels + 1, axis=1)
    blocks = {
        1 << level: jnp.concatenate([act, term.astype(jnp.bfloat16)], axis=1)
        for level, term in enumerate(terms)
    }
    latents, fars, (act, grad) = sum_over_hid(part, blocks, (act, grad))
    latent, dlatent = latents[:, :rank], latents[:, rank:]

    acts = [act] + [far[:, :side] for far in fars]
    total = dot(act, butterfly[0, 0])
    for level in range(1, levels + 1):
        total = total + dot(acts[level], butterfly[0, level])
        back = back + fars[level - 1][:, side:].astype(jnp.float32)

    output_rows = (total + dot(latent, low_v)).astype(jnp.bfloat16)
    grad_act = (back + dot_t(dlatent, low_u)).astype(jnp.bfloat16)
    grad_pre_rows = pullback(grad_act.astype(jnp.float32))[0].astype(jnp.bfloat16)
    results = jnp.concatenate([output_rows, grad_pre_rows], axis=1)
    results = lax.all_to_all(results, "hid", split_axis=0, concat_axis=1, tiled=True)
    results = results.reshape(tokens, hid, 2 * side)
    output = results[:, :, :side].reshape(tokens, hid * side)
    grad_pre = results[:, :, side:].reshape(tokens, hid * side)

    split = [halves(x, first) for x in acts[1:]]
    got = mate(jnp.concatenate([grad, act] + [theirs for ours, theirs in split[::-1]], axis=1))
    far_grad, far_act = got[:, :side], got[:, side : 2 * side]
    far_halves = jnp.split(got[:, 2 * side :], levels, axis=1)[::-1]
    latent, sent_latent = halves(latent, first)
    dlatent, sent_dlatent = halves(dlatent, first)
    got = mate(jnp.concatenate([sent_latent, sent_dlatent], axis=1))

    def tokens_of(own, far):
        return jnp.concatenate([own, far], axis=0)

    grads = tokens_of(grad, far_grad)
    own = jnp.concatenate([halves(act, first)[0]] + [ours for ours, theirs in split], axis=1)
    far = jnp.concatenate([halves(far_act, first)[0]] + far_halves, axis=1)
    grad_butterfly = inner_rows(tokens_of(own, far), grads) * factor
    grad_butterfly = grad_butterfly.reshape(1, levels + 1, side // 2, side)
    got, grad_butterfly = lax.optimization_barrier((got, grad_butterfly))
    grad_low_u = inner_rows(tokens_of(act, far_act), tokens_of(dlatent, got[:, rank // 2 :])) * factor
    grad_low_v = inner_rows(tokens_of(latent, got[:, : rank // 2]), grads) * factor
    return (output, grad_pre, grad_butterfly, grad_low_u, grad_low_v)


def solution(mesh):
    in_specs = (
        P(("hid", "seq"), None),
        P("hid", None, None, None),
        P("hid", None),
        P(None, "hid"),
        P(("hid", "seq"), None),
    )
    out_specs = (
        P(("hid", "seq"), None),
        P(("hid", "seq"), None),
        P("hid", None, "seq", None),
        P("hid", "seq"),
        P("seq", "hid"),
    )
    return jax.shard_map(
        on_device, mesh=mesh, in_specs=in_specs, out_specs=out_specs, check_vma=False
    )
```

```python
import math

import jax
import jax.numpy as jnp
from jax import lax
from jax.sharding import PartitionSpec as P


def exchange(x, mask):
    return lax.ppermute(x, "hid", [(i, i ^ mask) for i in range(lax.axis_size("hid"))])


def mate(x):
    return lax.ppermute(x, "seq", [(0, 1), (1, 0)])


def gelu_tanh(value):
    return jax.nn.gelu(value, approximate=True)


def dot(left, right):
    return jnp.dot(left, right, preferred_element_type=jnp.float32)


def dot_t(left, right):
    return lax.dot_general(
        left, right, (((1,), (1,)), ((), ())), preferred_element_type=jnp.float32
    )


def inner_rows(left, right):
    return lax.dot_general(
        left, right, (((0,), (0,)), ((), ())), preferred_element_type=jnp.float32
    )


def sum_over_hid(part, blocks, data):
    bits = (lax.axis_size("hid") - 1).bit_length()
    rounds = [(3, 1, 2)] + [(1 << bit,) for bit in range(2, bits)]
    total, far = part, {}
    for at, masks in enumerate(rounds):
        sent = total.astype(jnp.bfloat16)
        if at == 0:
            beside = {max(blocks): blocks[max(blocks)]}
        elif at == 1:
            early, beside = far, {mask: blocks[mask] for mask in blocks if mask not in far}
            sent, beside = lax.optimization_barrier((sent, beside))
        else:
            beside = {}
        if at == len(rounds) - 1:
            sent, data = lax.optimization_barrier((sent, data))
        got = [exchange(sent, mask) for mask in masks]
        far = far | {mask: exchange(beside[mask], mask) for mask in beside}
        if at == 1:
            got, blocks_early = lax.optimization_barrier((got, list(early.values())))
            far = far | dict(zip(early, blocks_early))
        else:
            got = lax.optimization_barrier(got)
        total = total + sum(x.astype(jnp.float32) for x in got)
    return total.astype(jnp.bfloat16), [far[mask] for mask in blocks], data


def halves(x, first):
    width = x.shape[1] // 2
    low, high = x[:, :width], x[:, width:]
    return jnp.where(first, low, high), jnp.where(first, high, low)


def on_device(pre_act, butterfly, low_u, low_v, grad_out):
    tokens = pre_act.shape[0]
    hid = lax.axis_size("hid")
    first = lax.axis_index("seq") == 0
    side = butterfly.shape[-1]
    levels = butterfly.shape[1] - 1
    rank = low_u.shape[1]
    factor = 1.0 / math.sqrt(tokens * hid * lax.axis_size("seq"))

    pre_act, grad_out, first = lax.optimization_barrier((pre_act, grad_out, first))
    both = jnp.concatenate(
        [pre_act.reshape(tokens, hid, side), grad_out.reshape(tokens, hid, side)], axis=2
    ).reshape(tokens, hid * 2 * side)
    rows = lax.all_to_all(both, "hid", split_axis=1, concat_axis=0, tiled=True)
    pre_f = rows[:, :side].astype(jnp.float32)
    grad = rows[:, side:]
    act_f, pullback = jax.vjp(gelu_tanh, pre_f)
    act = act_f.astype(jnp.bfloat16)

    part = jnp.concatenate([dot(act, low_u), dot_t(grad, low_v)], axis=1)
    terms = dot_t(grad, butterfly.reshape((levels + 1) * side, side))
    back, *terms = jnp.split(terms, levels + 1, axis=1)
    blocks = {
        1 << level: jnp.concatenate([act, term.astype(jnp.bfloat16)], axis=1)
        for level, term in enumerate(terms)
    }
    latents, fars, (act, grad) = sum_over_hid(part, blocks, (act, grad))
    latent, dlatent = latents[:, :rank], latents[:, rank:]

    acts = [act] + [far[:, :side] for far in fars]
    total = dot(act, butterfly[0, 0])
    for level in range(1, levels + 1):
        total = total + dot(acts[level], butterfly[0, level])
        back = back + fars[level - 1][:, side:].astype(jnp.float32)

    output_rows = (total + dot(latent, low_v)).astype(jnp.bfloat16)
    grad_act = (back + dot_t(dlatent, low_u)).astype(jnp.bfloat16)
    grad_pre_rows = pullback(grad_act.astype(jnp.float32))[0].astype(jnp.bfloat16)
    results = jnp.concatenate([output_rows, grad_pre_rows], axis=1)
    results = lax.all_to_all(results, "hid", split_axis=0, concat_axis=1, tiled=True)
    results = results.reshape(tokens, hid, 2 * side)
    output = results[:, :, :side].reshape(tokens, hid * side)
    grad_pre = results[:, :, side:].reshape(tokens, hid * side)

    split = [halves(x, first) for x in acts[1:]]
    got = mate(jnp.concatenate([grad, act] + [theirs for ours, theirs in split[::-1]], axis=1))
    far_grad, far_act = got[:, :side], got[:, side : 2 * side]
    far_halves = jnp.split(got[:, 2 * side :], levels, axis=1)[::-1]
    latent, sent_latent = halves(latent, first)
    dlatent, sent_dlatent = halves(dlatent, first)
    got = mate(jnp.concatenate([sent_latent, sent_dlatent], axis=1))

    def tokens_of(own, far):
        return jnp.concatenate([own, far], axis=0)

    grads = tokens_of(grad, far_grad)
    own = jnp.concatenate([halves(act, first)[0]] + [ours for ours, theirs in split], axis=1)
    far = jnp.concatenate([halves(far_act, first)[0]] + far_halves, axis=1)
    grad_butterfly = inner_rows(tokens_of(own, far), grads) * factor
    grad_butterfly = grad_butterfly.reshape(1, levels + 1, side // 2, side)
    got, grad_butterfly = lax.optimization_barrier((got, grad_butterfly))
    grad_low_u = inner_rows(tokens_of(act, far_act), tokens_of(dlatent, got[:, rank // 2 :])) * factor
    grad_low_v = inner_rows(tokens_of(latent, got[:, : rank // 2]), grads) * factor
    return (output, grad_pre, grad_butterfly, grad_low_u, grad_low_v)


def solution(mesh):
    in_specs = (
        P(("hid", "seq"), None),
        P("hid", None, None, None),
        P("hid", None),
        P(None, "hid"),
        P(("hid", "seq"), None),
    )
    out_specs = (
        P(("hid", "seq"), None),
        P(("hid", "seq"), None),
        P("hid", None, "seq", None),
        P("hid", "seq"),
        P("seq", "hid"),
    )
    return jax.shard_map(
        on_device, mesh=mesh, in_specs=in_specs, out_specs=out_specs, check_vma=False
    )
```

```python
import math

import jax
import jax.numpy as jnp
from jax import lax
from jax.sharding import PartitionSpec as P


def exchange(x, mask):
    return lax.ppermute(x, "hid", [(i, i ^ mask) for i in range(lax.axis_size("hid"))])


def mate(x):
    return lax.ppermute(x, "seq", [(0, 1), (1, 0)])


def gelu_tanh(value):
    return jax.nn.gelu(value, approximate=True)


def dot(left, right):
    return jnp.dot(left, right, preferred_element_type=jnp.float32)


def dot_t(left, right):
    return lax.dot_general(
        left, right, (((1,), (1,)), ((), ())), preferred_element_type=jnp.float32
    )


def inner_rows(left, right):
    return lax.dot_general(
        left, right, (((0,), (0,)), ((), ())), preferred_element_type=jnp.float32
    )


def sum_over_hid(part, blocks, data):
    bits = (lax.axis_size("hid") - 1).bit_length()
    rounds = [(5, 1, 4), (10, 8, 2)] + [(1 << bit,) for bit in range(4, bits)]
    total, far = part, {}
    for at, masks in enumerate(rounds):
        sent = total.astype(jnp.bfloat16)
        if at == 0:
            beside = {max(blocks): blocks[max(blocks)]}
        elif at == 1:
            early, beside = far, {mask: blocks[mask] for mask in blocks if mask not in far}
            sent, beside = lax.optimization_barrier((sent, beside))
        else:
            beside = {}
        if at == len(rounds) - 1:
            sent, data = lax.optimization_barrier((sent, data))
        got = [exchange(sent, mask) for mask in masks]
        far = far | {mask: exchange(beside[mask], mask) for mask in beside}
        if at == 1:
            got, blocks_early = lax.optimization_barrier((got, list(early.values())))
            far = far | dict(zip(early, blocks_early))
        else:
            got = lax.optimization_barrier(got)
        total = total + sum(x.astype(jnp.float32) for x in got)
    return total.astype(jnp.bfloat16), [far[mask] for mask in blocks], data


def halves(x, first):
    width = x.shape[1] // 2
    low, high = x[:, :width], x[:, width:]
    return jnp.where(first, low, high), jnp.where(first, high, low)


def on_device(pre_act, butterfly, low_u, low_v, grad_out):
    tokens = pre_act.shape[0]
    hid = lax.axis_size("hid")
    first = lax.axis_index("seq") == 0
    side = butterfly.shape[-1]
    levels = butterfly.shape[1] - 1
    rank = low_u.shape[1]
    factor = 1.0 / math.sqrt(tokens * hid * lax.axis_size("seq"))

    pre_act, grad_out, first = lax.optimization_barrier((pre_act, grad_out, first))
    both = jnp.concatenate(
        [pre_act.reshape(tokens, hid, side), grad_out.reshape(tokens, hid, side)], axis=2
    ).reshape(tokens, hid * 2 * side)
    rows = lax.all_to_all(both, "hid", split_axis=1, concat_axis=0, tiled=True)
    pre_f = rows[:, :side].astype(jnp.float32)
    grad = rows[:, side:]
    act_f, pullback = jax.vjp(gelu_tanh, pre_f)
    act = act_f.astype(jnp.bfloat16)

    part = jnp.concatenate([dot(act, low_u), dot_t(grad, low_v)], axis=1)
    terms = dot_t(grad, butterfly.reshape((levels + 1) * side, side))
    back, *terms = jnp.split(terms, levels + 1, axis=1)
    blocks = {
        1 << level: jnp.concatenate([act, term.astype(jnp.bfloat16)], axis=1)
        for level, term in enumerate(terms)
    }
    latents, fars, (act, grad) = sum_over_hid(part, blocks, (act, grad))
    latent, dlatent = latents[:, :rank], latents[:, rank:]

    acts = [act] + [far[:, :side] for far in fars]
    total = dot(act, butterfly[0, 0])
    for level in range(1, levels + 1):
        total = total + dot(acts[level], butterfly[0, level])
        back = back + fars[level - 1][:, side:].astype(jnp.float32)

    output_rows = (total + dot(latent, low_v)).astype(jnp.bfloat16)
    grad_act = (back + dot_t(dlatent, low_u)).astype(jnp.bfloat16)
    grad_pre_rows = pullback(grad_act.astype(jnp.float32))[0].astype(jnp.bfloat16)
    results = jnp.concatenate([output_rows, grad_pre_rows], axis=1)
    results = lax.all_to_all(results, "hid", split_axis=0, concat_axis=1, tiled=True)
    results = results.reshape(tokens, hid, 2 * side)
    output = results[:, :, :side].reshape(tokens, hid * side)
    grad_pre = results[:, :, side:].reshape(tokens, hid * side)

    split = [halves(x, first) for x in acts[1:]]
    got = mate(jnp.concatenate([grad, act] + [theirs for ours, theirs in split[::-1]], axis=1))
    far_grad, far_act = got[:, :side], got[:, side : 2 * side]
    far_halves = jnp.split(got[:, 2 * side :], levels, axis=1)[::-1]
    latent, sent_latent = halves(latent, first)
    dlatent, sent_dlatent = halves(dlatent, first)
    got = mate(jnp.concatenate([sent_latent, sent_dlatent], axis=1))

    def tokens_of(own, far):
        return jnp.concatenate([own, far], axis=0)

    grads = tokens_of(grad, far_grad)
    own = jnp.concatenate([halves(act, first)[0]] + [ours for ours, theirs in split], axis=1)
    far = jnp.concatenate([halves(far_act, first)[0]] + far_halves, axis=1)
    grad_butterfly = inner_rows(tokens_of(own, far), grads) * factor
    grad_butterfly = grad_butterfly.reshape(1, levels + 1, side // 2, side)
    got, grad_butterfly = lax.optimization_barrier((got, grad_butterfly))
    grad_low_u = inner_rows(tokens_of(act, far_act), tokens_of(dlatent, got[:, rank // 2 :])) * factor
    grad_low_v = inner_rows(tokens_of(latent, got[:, : rank // 2]), grads) * factor
    return (output, grad_pre, grad_butterfly, grad_low_u, grad_low_v)


def solution(mesh):
    in_specs = (
        P(("hid", "seq"), None),
        P("hid", None, None, None),
        P("hid", None),
        P(None, "hid"),
        P(("hid", "seq"), None),
    )
    out_specs = (
        P(("hid", "seq"), None),
        P(("hid", "seq"), None),
        P("hid", None, "seq", None),
        P("hid", "seq"),
        P("seq", "hid"),
    )
    return jax.shard_map(
        on_device, mesh=mesh, in_specs=in_specs, out_specs=out_specs, check_vma=False
    )
```

```python
import math

import jax
import jax.numpy as jnp
from jax import lax
from jax.sharding import PartitionSpec as P


def exchange(x, mask):
    return lax.ppermute(x, "hid", [(i, i ^ mask) for i in range(lax.axis_size("hid"))])


def mate(x):
    return lax.ppermute(x, "seq", [(0, 1), (1, 0)])


def gelu_tanh(value):
    return jax.nn.gelu(value, approximate=True)


def dot(left, right):
    return jnp.dot(left, right, preferred_element_type=jnp.float32)


def dot_t(left, right):
    return lax.dot_general(
        left, right, (((1,), (1,)), ((), ())), preferred_element_type=jnp.float32
    )


def inner_rows(left, right):
    return lax.dot_general(
        left, right, (((0,), (0,)), ((), ())), preferred_element_type=jnp.float32
    )


def sum_over_hid(part, blocks, data):
    bits = (lax.axis_size("hid") - 1).bit_length()
    rounds = [(3, 2, 1)] + [(1 << bit,) for bit in range(2, bits)]
    total, far = part, {}
    for at, masks in enumerate(rounds):
        sent = total.astype(jnp.bfloat16)
        if at == 0:
            beside = {mask: blocks[mask] for mask in sorted(blocks, reverse=True) if mask > 3}
        elif at == 1:
            early, beside = far, {mask: blocks[mask] for mask in blocks if mask not in far}
            sent, beside = lax.optimization_barrier((sent, beside))
        else:
            beside = {}
        if at == len(rounds) - 1:
            sent, data = lax.optimization_barrier((sent, data))
        got = [exchange(sent, mask) for mask in masks]
        far = far | {mask: exchange(beside[mask], mask) for mask in beside}
        if at == 1:
            got, early = lax.optimization_barrier((got, early))
            far = far | early
        else:
            got = lax.optimization_barrier(got)
        total = total + sum(x.astype(jnp.float32) for x in got)
    return total.astype(jnp.bfloat16), [far[mask] for mask in blocks], data


def halves(x, first):
    width = x.shape[1] // 2
    low, high = x[:, :width], x[:, width:]
    return jnp.where(first, low, high), jnp.where(first, high, low)


def on_device(pre_act, butterfly, low_u, low_v, grad_out):
    tokens = pre_act.shape[0]
    hid = lax.axis_size("hid")
    first = lax.axis_index("seq") == 0
    side = butterfly.shape[-1]
    levels = butterfly.shape[1] - 1
    rank = low_u.shape[1]
    factor = 1.0 / math.sqrt(tokens * hid * lax.axis_size("seq"))

    pre_act, grad_out, first = lax.optimization_barrier((pre_act, grad_out, first))
    both = jnp.concatenate(
        [pre_act.reshape(tokens, hid, side), grad_out.reshape(tokens, hid, side)], axis=2
    ).reshape(tokens, hid * 2 * side)
    rows = lax.all_to_all(both, "hid", split_axis=1, concat_axis=0, tiled=True)
    pre_f = rows[:, :side].astype(jnp.float32)
    grad = rows[:, side:]
    act_f, pullback = jax.vjp(gelu_tanh, pre_f)
    act = act_f.astype(jnp.bfloat16)

    part = jnp.concatenate([dot(act, low_u), dot_t(grad, low_v)], axis=1)
    terms = dot_t(grad, butterfly.reshape((levels + 1) * side, side))
    back, *terms = jnp.split(terms, levels + 1, axis=1)
    blocks = {
        1 << level: jnp.concatenate([act, term.astype(jnp.bfloat16)], axis=1)
        for level, term in enumerate(terms)
    }
    latents, fars, (act, grad) = sum_over_hid(part, blocks, (act, grad))
    latent, dlatent = latents[:, :rank], latents[:, rank:]

    acts = [act] + [far[:, :side] for far in fars]
    total = dot(act, butterfly[0, 0])
    for level in range(1, levels + 1):
        total = total + dot(acts[level], butterfly[0, level])
        back = back + fars[level - 1][:, side:].astype(jnp.float32)

    output_rows = (total + dot(latent, low_v)).astype(jnp.bfloat16)
    grad_act = (back + dot_t(dlatent, low_u)).astype(jnp.bfloat16)
    grad_pre_rows = pullback(grad_act.astype(jnp.float32))[0].astype(jnp.bfloat16)
    results = jnp.concatenate([output_rows, grad_pre_rows], axis=1)
    results = lax.all_to_all(results, "hid", split_axis=0, concat_axis=1, tiled=True)
    results = results.reshape(tokens, hid, 2 * side)
    output = results[:, :, :side].reshape(tokens, hid * side)
    grad_pre = results[:, :, side:].reshape(tokens, hid * side)

    split = [halves(x, first) for x in acts[1:]]
    got = mate(jnp.concatenate([grad, act] + [theirs for ours, theirs in split[::-1]], axis=1))
    far_grad, far_act = got[:, :side], got[:, side : 2 * side]
    far_halves = jnp.split(got[:, 2 * side :], levels, axis=1)[::-1]
    latent, sent_latent = halves(latent, first)
    dlatent, sent_dlatent = halves(dlatent, first)
    got = mate(jnp.concatenate([sent_latent, sent_dlatent], axis=1))

    def tokens_of(own, far):
        return jnp.concatenate([own, far], axis=0)

    grads = tokens_of(grad, far_grad)
    own = jnp.concatenate([halves(act, first)[0]] + [ours for ours, theirs in split], axis=1)
    far = jnp.concatenate([halves(far_act, first)[0]] + far_halves, axis=1)
    grad_butterfly = inner_rows(tokens_of(own, far), grads) * factor
    grad_butterfly = grad_butterfly.reshape(1, levels + 1, side // 2, side)
    got, grad_butterfly = lax.optimization_barrier((got, grad_butterfly))
    grad_low_u = inner_rows(tokens_of(act, far_act), tokens_of(dlatent, got[:, rank // 2 :])) * factor
    grad_low_v = inner_rows(tokens_of(latent, got[:, : rank // 2]), grads) * factor
    return (output, grad_pre, grad_butterfly, grad_low_u, grad_low_v)


def solution(mesh):
    in_specs = (
        P(("hid", "seq"), None),
        P("hid", None, None, None),
        P("hid", None),
        P(None, "hid"),
        P(("hid", "seq"), None),
    )
    out_specs = (
        P(("hid", "seq"), None),
        P(("hid", "seq"), None),
        P("hid", None, "seq", None),
        P("hid", "seq"),
        P("seq", "hid"),
    )
    return jax.shard_map(
        on_device, mesh=mesh, in_specs=in_specs, out_specs=out_specs, check_vma=False
    )
```

```python
import math

import jax
import jax.numpy as jnp
from jax import lax
from jax.sharding import PartitionSpec as P


def exchange(x, mask):
    return lax.ppermute(x, "hid", [(i, i ^ mask) for i in range(lax.axis_size("hid"))])


def mate(x):
    return lax.ppermute(x, "seq", [(0, 1), (1, 0)])


def gelu_tanh(value):
    return jax.nn.gelu(value, approximate=True)


def dot(left, right):
    return jnp.dot(left, right, preferred_element_type=jnp.float32)


def dot_t(left, right):
    return lax.dot_general(
        left, right, (((1,), (1,)), ((), ())), preferred_element_type=jnp.float32
    )


def inner_rows(left, right):
    return lax.dot_general(
        left, right, (((0,), (0,)), ((), ())), preferred_element_type=jnp.float32
    )


def sum_over_hid(part, blocks, data):
    bits = (lax.axis_size("hid") - 1).bit_length()
    rounds = [(3, 2, 1)] + [(1 << bit,) for bit in range(2, bits)]
    total, far = part, {}
    for at, masks in enumerate(rounds):
        sent = total.astype(jnp.bfloat16)
        if at == 0:
            beside = {mask: blocks[mask] for mask in blocks if 3 < mask < max(blocks)}
        elif at == 1:
            early, beside = far, {mask: blocks[mask] for mask in blocks if mask not in far}
            sent, beside = lax.optimization_barrier((sent, beside))
        else:
            beside = {}
        if at == len(rounds) - 1:
            sent, data = lax.optimization_barrier((sent, data))
        got = [exchange(sent, mask) for mask in masks]
        far = far | {mask: exchange(beside[mask], mask) for mask in beside}
        if at == 1:
            got, early = lax.optimization_barrier((got, early))
            far = far | early
        else:
            got = lax.optimization_barrier(got)
        total = total + sum(x.astype(jnp.float32) for x in got)
    return total.astype(jnp.bfloat16), [far[mask] for mask in blocks], data


def halves(x, first):
    width = x.shape[1] // 2
    low, high = x[:, :width], x[:, width:]
    return jnp.where(first, low, high), jnp.where(first, high, low)


def on_device(pre_act, butterfly, low_u, low_v, grad_out):
    tokens = pre_act.shape[0]
    hid = lax.axis_size("hid")
    first = lax.axis_index("seq") == 0
    side = butterfly.shape[-1]
    levels = butterfly.shape[1] - 1
    rank = low_u.shape[1]
    factor = 1.0 / math.sqrt(tokens * hid * lax.axis_size("seq"))

    pre_act, grad_out, first = lax.optimization_barrier((pre_act, grad_out, first))
    both = jnp.concatenate(
        [pre_act.reshape(tokens, hid, side), grad_out.reshape(tokens, hid, side)], axis=2
    ).reshape(tokens, hid * 2 * side)
    rows = lax.all_to_all(both, "hid", split_axis=1, concat_axis=0, tiled=True)
    pre_f = rows[:, :side].astype(jnp.float32)
    grad = rows[:, side:]
    act_f, pullback = jax.vjp(gelu_tanh, pre_f)
    act = act_f.astype(jnp.bfloat16)

    part = jnp.concatenate([dot(act, low_u), dot_t(grad, low_v)], axis=1)
    terms = dot_t(grad, butterfly.reshape((levels + 1) * side, side))
    back, *terms = jnp.split(terms, levels + 1, axis=1)
    blocks = {
        1 << level: jnp.concatenate([act, term.astype(jnp.bfloat16)], axis=1)
        for level, term in enumerate(terms)
    }
    latents, fars, (act, grad) = sum_over_hid(part, blocks, (act, grad))
    latent, dlatent = latents[:, :rank], latents[:, rank:]

    acts = [act] + [far[:, :side] for far in fars]
    total = dot(act, butterfly[0, 0])
    for level in range(1, levels + 1):
        total = total + dot(acts[level], butterfly[0, level])
        back = back + fars[level - 1][:, side:].astype(jnp.float32)

    output_rows = (total + dot(latent, low_v)).astype(jnp.bfloat16)
    grad_act = (back + dot_t(dlatent, low_u)).astype(jnp.bfloat16)
    grad_pre_rows = pullback(grad_act.astype(jnp.float32))[0].astype(jnp.bfloat16)
    results = jnp.concatenate([output_rows, grad_pre_rows], axis=1)
    results = lax.all_to_all(results, "hid", split_axis=0, concat_axis=1, tiled=True)
    results = results.reshape(tokens, hid, 2 * side)
    output = results[:, :, :side].reshape(tokens, hid * side)
    grad_pre = results[:, :, side:].reshape(tokens, hid * side)

    split = [halves(x, first) for x in acts[1:]]
    got = mate(jnp.concatenate([grad, act] + [theirs for ours, theirs in split[::-1]], axis=1))
    far_grad, far_act = got[:, :side], got[:, side : 2 * side]
    far_halves = jnp.split(got[:, 2 * side :], levels, axis=1)[::-1]
    latent, sent_latent = halves(latent, first)
    dlatent, sent_dlatent = halves(dlatent, first)
    got = mate(jnp.concatenate([sent_latent, sent_dlatent], axis=1))

    def tokens_of(own, far):
        return jnp.concatenate([own, far], axis=0)

    grads = tokens_of(grad, far_grad)
    own = jnp.concatenate([halves(act, first)[0]] + [ours for ours, theirs in split], axis=1)
    far = jnp.concatenate([halves(far_act, first)[0]] + far_halves, axis=1)
    grad_butterfly = inner_rows(tokens_of(own, far), grads) * factor
    grad_butterfly = grad_butterfly.reshape(1, levels + 1, side // 2, side)
    got, grad_butterfly = lax.optimization_barrier((got, grad_butterfly))
    grad_low_u = inner_rows(tokens_of(act, far_act), tokens_of(dlatent, got[:, rank // 2 :])) * factor
    grad_low_v = inner_rows(tokens_of(latent, got[:, : rank // 2]), grads) * factor
    return (output, grad_pre, grad_butterfly, grad_low_u, grad_low_v)


def solution(mesh):
    in_specs = (
        P(("hid", "seq"), None),
        P("hid", None, None, None),
        P("hid", None),
        P(None, "hid"),
        P(("hid", "seq"), None),
    )
    out_specs = (
        P(("hid", "seq"), None),
        P(("hid", "seq"), None),
        P("hid", None, "seq", None),
        P("hid", "seq"),
        P("seq", "hid"),
    )
    return jax.shard_map(
        on_device, mesh=mesh, in_specs=in_specs, out_specs=out_specs, check_vma=False
    )
```

```python
import math

import jax
import jax.numpy as jnp
from jax import lax
from jax.sharding import PartitionSpec as P


def exchange(x, mask):
    return lax.ppermute(x, "hid", [(i, i ^ mask) for i in range(lax.axis_size("hid"))])


def mate(x):
    return lax.ppermute(x, "seq", [(0, 1), (1, 0)])


def gelu_tanh(value):
    return jax.nn.gelu(value, approximate=True)


def dot(left, right):
    return jnp.dot(left, right, preferred_element_type=jnp.float32)


def dot_t(left, right):
    return lax.dot_general(
        left, right, (((1,), (1,)), ((), ())), preferred_element_type=jnp.float32
    )


def inner_rows(left, right):
    return lax.dot_general(
        left, right, (((0,), (0,)), ((), ())), preferred_element_type=jnp.float32
    )


def sum_over_hid(part, blocks, data):
    bits = (lax.axis_size("hid") - 1).bit_length()
    rounds = [(3, 2, 1), (8,), (4,)] + [(1 << bit,) for bit in range(4, bits)]
    total, far = part, {}
    for at, masks in enumerate(rounds):
        sent = total.astype(jnp.bfloat16)
        if at == 0:
            beside = {mask: blocks[mask] for mask in blocks if 3 < mask < max(blocks)}
        elif at == 1:
            early, beside = far, {mask: blocks[mask] for mask in blocks if mask not in far}
            sent, beside = lax.optimization_barrier((sent, beside))
        else:
            beside = {}
        if at == len(rounds) - 1:
            sent, data = lax.optimization_barrier((sent, data))
        got = [exchange(sent, mask) for mask in masks]
        far = far | {mask: exchange(beside[mask], mask) for mask in beside}
        if at == 1:
            got, early = lax.optimization_barrier((got, early))
            far = far | early
        else:
            got = lax.optimization_barrier(got)
        total = total + sum(x.astype(jnp.float32) for x in got)
    return total.astype(jnp.bfloat16), [far[mask] for mask in blocks], data


def halves(x, first):
    width = x.shape[1] // 2
    low, high = x[:, :width], x[:, width:]
    return jnp.where(first, low, high), jnp.where(first, high, low)


def on_device(pre_act, butterfly, low_u, low_v, grad_out):
    tokens = pre_act.shape[0]
    hid = lax.axis_size("hid")
    first = lax.axis_index("seq") == 0
    side = butterfly.shape[-1]
    levels = butterfly.shape[1] - 1
    rank = low_u.shape[1]
    factor = 1.0 / math.sqrt(tokens * hid * lax.axis_size("seq"))

    pre_act, grad_out, first = lax.optimization_barrier((pre_act, grad_out, first))
    both = jnp.concatenate(
        [pre_act.reshape(tokens, hid, side), grad_out.reshape(tokens, hid, side)], axis=2
    ).reshape(tokens, hid * 2 * side)
    rows = lax.all_to_all(both, "hid", split_axis=1, concat_axis=0, tiled=True)
    pre_f = rows[:, :side].astype(jnp.float32)
    grad = rows[:, side:]
    act_f, pullback = jax.vjp(gelu_tanh, pre_f)
    act = act_f.astype(jnp.bfloat16)

    part = jnp.concatenate([dot(act, low_u), dot_t(grad, low_v)], axis=1)
    terms = dot_t(grad, butterfly.reshape((levels + 1) * side, side))
    back, *terms = jnp.split(terms, levels + 1, axis=1)
    blocks = {
        1 << level: jnp.concatenate([act, term.astype(jnp.bfloat16)], axis=1)
        for level, term in enumerate(terms)
    }
    latents, fars, (act, grad) = sum_over_hid(part, blocks, (act, grad))
    latent, dlatent = latents[:, :rank], latents[:, rank:]

    acts = [act] + [far[:, :side] for far in fars]
    total = dot(act, butterfly[0, 0])
    for level in range(1, levels + 1):
        total = total + dot(acts[level], butterfly[0, level])
        back = back + fars[level - 1][:, side:].astype(jnp.float32)

    output_rows = (total + dot(latent, low_v)).astype(jnp.bfloat16)
    grad_act = (back + dot_t(dlatent, low_u)).astype(jnp.bfloat16)
    grad_pre_rows = pullback(grad_act.astype(jnp.float32))[0].astype(jnp.bfloat16)
    results = jnp.concatenate([output_rows, grad_pre_rows], axis=1)
    results = lax.all_to_all(results, "hid", split_axis=0, concat_axis=1, tiled=True)
    results = results.reshape(tokens, hid, 2 * side)
    output = results[:, :, :side].reshape(tokens, hid * side)
    grad_pre = results[:, :, side:].reshape(tokens, hid * side)

    split = [halves(x, first) for x in acts[1:]]
    got = mate(jnp.concatenate([grad, act] + [theirs for ours, theirs in split[::-1]], axis=1))
    far_grad, far_act = got[:, :side], got[:, side : 2 * side]
    far_halves = jnp.split(got[:, 2 * side :], levels, axis=1)[::-1]
    latent, sent_latent = halves(latent, first)
    dlatent, sent_dlatent = halves(dlatent, first)
    got = mate(jnp.concatenate([sent_latent, sent_dlatent], axis=1))

    def tokens_of(own, far):
        return jnp.concatenate([own, far], axis=0)

    grads = tokens_of(grad, far_grad)
    own = jnp.concatenate([halves(act, first)[0]] + [ours for ours, theirs in split], axis=1)
    far = jnp.concatenate([halves(far_act, first)[0]] + far_halves, axis=1)
    grad_butterfly = inner_rows(tokens_of(own, far), grads) * factor
    grad_butterfly = grad_butterfly.reshape(1, levels + 1, side // 2, side)
    got, grad_butterfly = lax.optimization_barrier((got, grad_butterfly))
    grad_low_u = inner_rows(tokens_of(act, far_act), tokens_of(dlatent, got[:, rank // 2 :])) * factor
    grad_low_v = inner_rows(tokens_of(latent, got[:, : rank // 2]), grads) * factor
    return (output, grad_pre, grad_butterfly, grad_low_u, grad_low_v)


def solution(mesh):
    in_specs = (
        P(("hid", "seq"), None),
        P("hid", None, None, None),
        P("hid", None),
        P(None, "hid"),
        P(("hid", "seq"), None),
    )
    out_specs = (
        P(("hid", "seq"), None),
        P(("hid", "seq"), None),
        P("hid", None, "seq", None),
        P("hid", "seq"),
        P("seq", "hid"),
    )
    return jax.shard_map(
        on_device, mesh=mesh, in_specs=in_specs, out_specs=out_specs, check_vma=False
    )
```

```python
import math

import jax
import jax.numpy as jnp
from jax import lax
from jax.sharding import PartitionSpec as P


def exchange(x, mask):
    return lax.ppermute(x, "hid", [(i, i ^ mask) for i in range(lax.axis_size("hid"))])


def mate(x):
    return lax.ppermute(x, "seq", [(0, 1), (1, 0)])


def gelu_tanh(value):
    return jax.nn.gelu(value, approximate=True)


def dot(left, right):
    return jnp.dot(left, right, preferred_element_type=jnp.float32)


def dot_t(left, right):
    return lax.dot_general(
        left, right, (((1,), (1,)), ((), ())), preferred_element_type=jnp.float32
    )


def inner_rows(left, right):
    return lax.dot_general(
        left, right, (((0,), (0,)), ((), ())), preferred_element_type=jnp.float32
    )


def sum_over_hid(part, blocks, data):
    bits = (lax.axis_size("hid") - 1).bit_length()
    rounds = [(3, 2, 1)] + [(1 << bit,) for bit in range(2, bits)]
    total, far = part, {}
    for at, masks in enumerate(rounds):
        sent = total.astype(jnp.bfloat16)
        if at == 0:
            beside = {mask: blocks[mask] for mask in sorted(blocks, reverse=True) if mask > 3}
        elif at == 1:
            early, beside = far, {mask: blocks[mask] for mask in blocks if mask not in far}
            sent, beside = lax.optimization_barrier((sent, beside))
        else:
            beside = {}
        if at == len(rounds) - 1:
            sent, data = lax.optimization_barrier((sent, data))
        got = [exchange(sent, mask) for mask in masks]
        far = far | {mask: exchange(beside[mask], mask) for mask in beside}
        if at == len(rounds) - 1:
            got, early = lax.optimization_barrier((got, early))
            far = far | early
        else:
            got = lax.optimization_barrier(got)
        total = total + sum(x.astype(jnp.float32) for x in got)
    return total.astype(jnp.bfloat16), [far[mask] for mask in blocks], data


def halves(x, first):
    width = x.shape[1] // 2
    low, high = x[:, :width], x[:, width:]
    return jnp.where(first, low, high), jnp.where(first, high, low)


def on_device(pre_act, butterfly, low_u, low_v, grad_out):
    tokens = pre_act.shape[0]
    hid = lax.axis_size("hid")
    first = lax.axis_index("seq") == 0
    side = butterfly.shape[-1]
    levels = butterfly.shape[1] - 1
    rank = low_u.shape[1]
    factor = 1.0 / math.sqrt(tokens * hid * lax.axis_size("seq"))

    pre_act, grad_out, first = lax.optimization_barrier((pre_act, grad_out, first))
    both = jnp.concatenate(
        [pre_act.reshape(tokens, hid, side), grad_out.reshape(tokens, hid, side)], axis=2
    ).reshape(tokens, hid * 2 * side)
    rows = lax.all_to_all(both, "hid", split_axis=1, concat_axis=0, tiled=True)
    pre_f = rows[:, :side].astype(jnp.float32)
    grad = rows[:, side:]
    act_f, pullback = jax.vjp(gelu_tanh, pre_f)
    act = act_f.astype(jnp.bfloat16)

    part = jnp.concatenate([dot(act, low_u), dot_t(grad, low_v)], axis=1)
    terms = dot_t(grad, butterfly.reshape((levels + 1) * side, side))
    back, *terms = jnp.split(terms, levels + 1, axis=1)
    blocks = {
        1 << level: jnp.concatenate([act, term.astype(jnp.bfloat16)], axis=1)
        for level, term in enumerate(terms)
    }
    latents, fars, (act, grad) = sum_over_hid(part, blocks, (act, grad))
    latent, dlatent = latents[:, :rank], latents[:, rank:]

    acts = [act] + [far[:, :side] for far in fars]
    total = dot(act, butterfly[0, 0])
    for level in range(1, levels + 1):
        total = total + dot(acts[level], butterfly[0, level])
        back = back + fars[level - 1][:, side:].astype(jnp.float32)

    output_rows = (total + dot(latent, low_v)).astype(jnp.bfloat16)
    grad_act = (back + dot_t(dlatent, low_u)).astype(jnp.bfloat16)
    grad_pre_rows = pullback(grad_act.astype(jnp.float32))[0].astype(jnp.bfloat16)
    results = jnp.concatenate([output_rows, grad_pre_rows], axis=1)
    results = lax.all_to_all(results, "hid", split_axis=0, concat_axis=1, tiled=True)
    results = results.reshape(tokens, hid, 2 * side)
    output = results[:, :, :side].reshape(tokens, hid * side)
    grad_pre = results[:, :, side:].reshape(tokens, hid * side)

    split = [halves(x, first) for x in acts[1:]]
    got = mate(jnp.concatenate([grad, act] + [theirs for ours, theirs in split[::-1]], axis=1))
    far_grad, far_act = got[:, :side], got[:, side : 2 * side]
    far_halves = jnp.split(got[:, 2 * side :], levels, axis=1)[::-1]
    latent, sent_latent = halves(latent, first)
    dlatent, sent_dlatent = halves(dlatent, first)
    got = mate(jnp.concatenate([sent_latent, sent_dlatent], axis=1))

    def tokens_of(own, far):
        return jnp.concatenate([own, far], axis=0)

    grads = tokens_of(grad, far_grad)
    own = jnp.concatenate([halves(act, first)[0]] + [ours for ours, theirs in split], axis=1)
    far = jnp.concatenate([halves(far_act, first)[0]] + far_halves, axis=1)
    grad_butterfly = inner_rows(tokens_of(own, far), grads) * factor
    grad_butterfly = grad_butterfly.reshape(1, levels + 1, side // 2, side)
    got, grad_butterfly = lax.optimization_barrier((got, grad_butterfly))
    grad_low_u = inner_rows(tokens_of(act, far_act), tokens_of(dlatent, got[:, rank // 2 :])) * factor
    grad_low_v = inner_rows(tokens_of(latent, got[:, : rank // 2]), grads) * factor
    return (output, grad_pre, grad_butterfly, grad_low_u, grad_low_v)


def solution(mesh):
    in_specs = (
        P(("hid", "seq"), None),
        P("hid", None, None, None),
        P("hid", None),
        P(None, "hid"),
        P(("hid", "seq"), None),
    )
    out_specs = (
        P(("hid", "seq"), None),
        P(("hid", "seq"), None),
        P("hid", None, "seq", None),
        P("hid", "seq"),
        P("seq", "hid"),
    )
    return jax.shard_map(
        on_device, mesh=mesh, in_specs=in_specs, out_specs=out_specs, check_vma=False
    )
```

```python
import math

import jax
import jax.numpy as jnp
from jax import lax
from jax.sharding import PartitionSpec as P


def exchange(x, mask):
    return lax.ppermute(x, "hid", [(i, i ^ mask) for i in range(lax.axis_size("hid"))])


def mate(x):
    return lax.ppermute(x, "seq", [(0, 1), (1, 0)])


def gelu_tanh(value):
    return jax.nn.gelu(value, approximate=True)


def dot(left, right):
    return jnp.dot(left, right, preferred_element_type=jnp.float32)


def dot_t(left, right):
    return lax.dot_general(
        left, right, (((1,), (1,)), ((), ())), preferred_element_type=jnp.float32
    )


def inner_rows(left, right):
    return lax.dot_general(
        left, right, (((0,), (0,)), ((), ())), preferred_element_type=jnp.float32
    )


def sum_over_hid(part, blocks, data):
    bits = (lax.axis_size("hid") - 1).bit_length()
    rounds = [(3, 1, 2)] + [(1 << bit,) for bit in range(2, bits)]
    total, far = part, {}
    for at, masks in enumerate(rounds):
        sent = total.astype(jnp.bfloat16)
        if at == 0:
            beside = {mask: blocks[mask] for mask in sorted(blocks, reverse=True) if mask > 3}
        elif at == 1:
            early, beside = far, {mask: blocks[mask] for mask in blocks if mask not in far}
            sent, beside = lax.optimization_barrier((sent, beside))
        else:
            beside = {}
        if at == len(rounds) - 1:
            sent, data = lax.optimization_barrier((sent, data))
        got = [exchange(sent, mask) for mask in masks]
        far = far | {mask: exchange(beside[mask], mask) for mask in beside}
        if at == 1:
            got, early = lax.optimization_barrier((got, early))
            far = far | early
        else:
            got = lax.optimization_barrier(got)
        total = total + sum(x.astype(jnp.float32) for x in got)
    return total.astype(jnp.bfloat16), [far[mask] for mask in blocks], data


def halves(x, first):
    width = x.shape[1] // 2
    low, high = x[:, :width], x[:, width:]
    return jnp.where(first, low, high), jnp.where(first, high, low)


def on_device(pre_act, butterfly, low_u, low_v, grad_out):
    tokens = pre_act.shape[0]
    hid = lax.axis_size("hid")
    first = lax.axis_index("seq") == 0
    side = butterfly.shape[-1]
    levels = butterfly.shape[1] - 1
    rank = low_u.shape[1]
    factor = 1.0 / math.sqrt(tokens * hid * lax.axis_size("seq"))

    pre_act, grad_out, first = lax.optimization_barrier((pre_act, grad_out, first))
    both = jnp.concatenate(
        [pre_act.reshape(tokens, hid, side), grad_out.reshape(tokens, hid, side)], axis=2
    ).reshape(tokens, hid * 2 * side)
    rows = lax.all_to_all(both, "hid", split_axis=1, concat_axis=0, tiled=True)
    pre_f = rows[:, :side].astype(jnp.float32)
    grad = rows[:, side:]
    act_f, pullback = jax.vjp(gelu_tanh, pre_f)
    act = act_f.astype(jnp.bfloat16)

    part = jnp.concatenate([dot(act, low_u), dot_t(grad, low_v)], axis=1)
    terms = dot_t(grad, butterfly.reshape((levels + 1) * side, side))
    back, *terms = jnp.split(terms, levels + 1, axis=1)
    blocks = {
        1 << level: jnp.concatenate([act, term.astype(jnp.bfloat16)], axis=1)
        for level, term in enumerate(terms)
    }
    latents, fars, (act, grad) = sum_over_hid(part, blocks, (act, grad))
    latent, dlatent = latents[:, :rank], latents[:, rank:]

    acts = [act] + [far[:, :side] for far in fars]
    total = dot(act, butterfly[0, 0])
    for level in range(1, levels + 1):
        total = total + dot(acts[level], butterfly[0, level])
        back = back + fars[level - 1][:, side:].astype(jnp.float32)

    output_rows = (total + dot(latent, low_v)).astype(jnp.bfloat16)
    grad_act = (back + dot_t(dlatent, low_u)).astype(jnp.bfloat16)
    grad_pre_rows = pullback(grad_act.astype(jnp.float32))[0].astype(jnp.bfloat16)
    results = jnp.concatenate(
        [x.reshape(hid, tokens, side) for x in (output_rows, grad_pre_rows)], axis=2
    )
    results = lax.all_to_all(results, "hid", 0, 0, tiled=True).transpose(1, 0, 2)
    results = results.reshape(tokens, hid, 2 * side)
    output = results[:, :, :side].reshape(tokens, hid * side)
    grad_pre = results[:, :, side:].reshape(tokens, hid * side)

    split = [halves(x, first) for x in acts[1:]]
    got = mate(jnp.concatenate([grad, act] + [theirs for ours, theirs in split[::-1]], axis=1))
    far_grad, far_act = got[:, :side], got[:, side : 2 * side]
    far_halves = jnp.split(got[:, 2 * side :], levels, axis=1)[::-1]
    latent, sent_latent = halves(latent, first)
    dlatent, sent_dlatent = halves(dlatent, first)
    got = mate(jnp.concatenate([sent_latent, sent_dlatent], axis=1))

    def tokens_of(own, far):
        return jnp.concatenate([own, far], axis=0)

    grads = tokens_of(grad, far_grad)
    own = jnp.concatenate([halves(act, first)[0]] + [ours for ours, theirs in split], axis=1)
    far = jnp.concatenate([halves(far_act, first)[0]] + far_halves, axis=1)
    grad_butterfly = inner_rows(tokens_of(own, far), grads) * factor
    grad_butterfly = grad_butterfly.reshape(1, levels + 1, side // 2, side)
    got, grad_butterfly = lax.optimization_barrier((got, grad_butterfly))
    grad_low_u = inner_rows(tokens_of(act, far_act), tokens_of(dlatent, got[:, rank // 2 :])) * factor
    grad_low_v = inner_rows(tokens_of(latent, got[:, : rank // 2]), grads) * factor
    return (output, grad_pre, grad_butterfly, grad_low_u, grad_low_v)


def solution(mesh):
    in_specs = (
        P(("hid", "seq"), None),
        P("hid", None, None, None),
        P("hid", None),
        P(None, "hid"),
        P(("hid", "seq"), None),
    )
    out_specs = (
        P(("hid", "seq"), None),
        P(("hid", "seq"), None),
        P("hid", None, "seq", None),
        P("hid", "seq"),
        P("seq", "hid"),
    )
    return jax.shard_map(
        on_device, mesh=mesh, in_specs=in_specs, out_specs=out_specs, check_vma=False
    )
```
